32 devices in a mesh: expert: 8 (over y, x, core), shard: 4 (over z).
Axes of the slice: x: 2, y: 2, z: 4, core: 2. Of those that a mesh axis runs over, the one named last changes fastest.
Arguments:
- tokens: bfloat16 [8192, 768], P(('expert', 'shard')), may hold values from -6 to 6
- w_query: bfloat16 [768, 768], P('shard'), may hold values from -0.21875 to 0.21875
- w_key: bfloat16 [768, 768], P('shard'), may hold values from -0.21875 to 0.21875
- w_value: bfloat16 [768, 768], P('shard'), may hold values from -0.21875 to 0.21875
- w_out_attn: bfloat16 [768, 768], P('shard'), may hold values from -2.5 to 2.5
- w_router: bfloat16 [768, 16], P('shard'), may hold values from -0.15625 to 0.15625
- gain_attn: bfloat16 [768], P('shard'), may hold values from 0.5 to 1.5
- gain_moe: bfloat16 [768], P('shard'), may hold values from 0.5 to 1.5
- rel_bias: bfloat16 [32, 12], P('shard'), may hold values from -3 to 3
- w_in: bfloat16 [16, 768, 3072], P('expert', None, 'shard'), may hold values from -0.21875 to 0.21875
- w_out: bfloat16 [16, 3072, 768], P('expert', 'shard'), may hold values from -0.109375 to 0.109375
- out_grad: bfloat16 [8192, 768], P(('expert', 'shard')), may hold values from -6 to 6
- routes: int32 [8192, 2], P(('expert', 'shard')), may hold values from 0 to 15, all different within a row; in each aligned block of 256 rows (0 to 255, 256 to 511, ...) at most 64 rows name the same one
- segments: int32 [8, 1024], P('expert'), may hold values from 0 to 2, as said below
- buckets: int32 [1024], replicated, may hold values from 0 to 31, as said below
Outputs:
- layer_out: bfloat16 [8192, 768], P(('expert', 'shard'))
- tokens_grad: bfloat16 [8192, 768], P(('expert', 'shard'))
- grad_w_query: float32 [768, 768], P('shard')
- grad_w_key: float32 [768, 768], P('shard')
- grad_w_value: float32 [768, 768], P('shard')
- grad_w_out_attn: float32 [768, 768], P('shard')
- grad_w_router: float32 [768, 16], P('shard')
- grad_gain_attn: float32 [768], P('shard')
- grad_gain_moe: float32 [768], P('shard')
- grad_rel_bias: float32 [32, 12], P('shard')
- grad_w_in: float32 [16, 768, 3072], P('expert', None, 'shard')
- grad_w_out: float32 [16, 3072, 768], P('expert', 'shard')
The draws below stay inside these ranges and needn't reach their ends.
Inputs may be any that keep to these rules, and one draw needn't show every extreme that they name: `routes`: the two experts of a token differ. Among the rows of one device no expert is named by more than 64 rows, a bound that some block reaches. `segments`: document numbers never fall along a sequence; each document is a run of consecutive tokens. Entry d is the bucket of the distance d between a query and an earlier key; buckets never fall as d grows, and distance 0 has bucket 0.
All inputs are finite; a program needn't handle non-finite values.
Results may differ from the reference program's by a relative error of at most 0.025.
Values may be sent and summed in bfloat16 or wider, within the bound.
A program may use at most 128 MiB of HBM per device.

```python
import math
import jax
import jax.numpy as jnp
import numpy as np
from jax import lax

D = 768
H = 12
FF = 3072
NB = 32
TOK_DEV = 256
EXPERT_TOTAL = 16
CAP = 64
L = 1024
SEQS = 8
TOKENS = 8192


def draw_segments(key, part):
    key = jax.random.fold_in(key, 11)
    subkeys = jax.random.split(key, 2)
    least_edge = max(1, TOK_DEV * 25 // 32)
    head_rows = jax.random.randint(subkeys[0], (SEQS, 1), least_edge, TOK_DEV)
    tail_rows = jax.random.randint(subkeys[1], (SEQS, 1), least_edge, TOK_DEV)
    places = jnp.arange(L, dtype=jnp.int32)[None, :]
    return ((places >= head_rows).astype(jnp.int32) + (places >= L - tail_rows).astype(jnp.int32)).astype(jnp.int32)


def draw_buckets(key, part):
    key = jax.random.fold_in(key, 23)
    exact = NB // 2
    marks = jax.random.randint(key, (NB - exact - 1,), exact + 1, L)
    distance = jnp.arange(L, dtype=jnp.int32)
    farther = exact + jnp.sum((distance[:, None] >= marks[None, :]).astype(jnp.int32), axis=1)
    return jnp.where(distance < exact, distance, farther).astype(jnp.int32)


def shard_levels(key, extent, cuts, low, top_value):
    factor_of, own = 1.0, jax.random.fold_in(key, 6)
    for axis_at, shards_of in cuts:
        steps = jnp.exp(jax.random.uniform(jax.random.fold_in(own, axis_at), (shards_of,), jnp.float32, low / len(cuts), top_value / len(cuts)))
        factor_of = factor_of * jnp.repeat(steps, extent[axis_at] // shards_of).reshape([-1 if axis == axis_at else 1 for axis in range(len(extent))])
    return factor_of


def routed_block(key, own, number, rows, amount, top, limit, slope):
    ranking = jax.random.permutation(key, amount)
    crowded, ordinary = portions_of(amount, rows * top, limit, slope, True), portions_of(amount, rows * top, limit, slope, False)
    places = jnp.arange(amount)

    def named(sizes, offset_by):
        used = int((sizes > 0).sum())
        fixed = max(1, used // 4)
        moved = fixed + (places - fixed + offset_by * (used - fixed)) % max(1, amount - fixed)
        return jnp.zeros((amount,), jnp.int32).at[ranking[jnp.where(places < fixed, places, moved)]].set(jnp.asarray(sizes, jnp.int32))

    sizes = jnp.where(number % 4 == 0, named(crowded, number // 4), named(ordinary, number - number // 4 - 1))
    mixed = jax.random.permutation(jax.random.fold_in(own, 3), amount)
    giver, receiver = mixed[0:amount // 2 * 2:2], mixed[1:amount // 2 * 2:2]
    margin = jnp.minimum(sizes[giver] - 1, limit - sizes[receiver]) // 2
    margin = jnp.where((giver == ranking[0]) | (receiver == ranking[0]) | (sizes[receiver] == 0), 0, jnp.maximum(margin, 0))
    moved = jax.random.randint(jax.random.fold_in(own, 4), (amount // 2,), 0, 1 << 20) % (margin + 1)
    sizes = sizes.at[giver].add(-moved).at[receiver].add(moved)
    members = jnp.searchsorted(jnp.cumsum(sizes), jnp.arange(rows * top), side="right").astype(jnp.int32)
    listing = members.reshape(top, rows).T
    listing = listing[jax.random.permutation(jax.random.fold_in(own, 1), rows)]
    offset_by = jax.random.randint(jax.random.fold_in(own, 2), (rows, 1), 0, top)
    return jnp.take_along_axis(listing, (jnp.arange(top)[None, :] + offset_by) % top, axis=1)


def portions_of(amount, total, limit, lean, full):
    portions = [(1 << 20) // math.isqrt(standing ** lean) + 1 for standing in range(1, amount + 1)]
    largest = limit if full else min(limit, max(-(-total // amount), total * portions[0] // sum(portions)))
    least = 1 if total - largest >= amount - 1 else 0
    holding, spare = [largest] + [least] * (amount - 1), total - largest - least * (amount - 1)
    while spare > 0:
        candidates = [i for i in range(1, amount) if holding[i] < largest] or [i for i in range(1, amount) if holding[i] < limit]
        mass, remaining = sum([portions[i] for i in candidates]), spare
        for i in candidates:
            extra = min(limit - holding[i], max(1, remaining * portions[i] // mass), spare)
            holding[i] = holding[i] + extra
            spare = spare - extra
    return np.array(holding)


def centred(key, shape, scale, limit, shards=(), held_as=jnp.bfloat16):
    entries = jax.random.normal(key, shape, jnp.float32) * scale
    if len(shards) > 0:
        entries = shard_levels(key, shape, shards, -0.22, 0.18) * entries
    return jnp.clip(entries, min=-limit, max=limit).astype(held_as)


def setup_inputs(seed: int = 0) -> dict:
    splits = jax.random.split(jax.random.key(seed), 16)
    tokens = centred(splits[0], (TOKENS, D), 1.0, 6.0, ((0, 32),))
    w_query = centred(splits[1], (D, D), D ** -0.5, 0.21875, ((0, 4),))
    w_key = centred(splits[2], (D, D), D ** -0.5, 0.21875, ((0, 4),))
    w_value = centred(splits[3], (D, D), D ** -0.5, 0.21875, ((0, 4),))
    w_out_attn = centred(splits[4], (D, D), (max(1, 8 * D // L)) ** -0.5, 2.5, ((0, 4),))
    w_router = centred(splits[5], (D, EXPERT_TOTAL), (2 * D) ** -0.5, 0.15625, ((0, 4),))
    gain_attn = jnp.clip(1.0 + 0.1 * jax.random.normal(splits[6], (D,), jnp.float32), 0.5, 1.5).astype(jnp.bfloat16)
    gain_moe = jnp.clip(1.0 + 0.1 * jax.random.normal(splits[7], (D,), jnp.float32), 0.5, 1.5).astype(jnp.bfloat16)
    rel_bias = centred(splits[8], (NB, H), 0.5, 3.0, ((0, 4),))
    w_in = centred(splits[9], (EXPERT_TOTAL, D, FF), D ** -0.5, 0.21875, ((0, 8), (2, 4)))
    w_out = centred(splits[10], (EXPERT_TOTAL, FF, D), FF ** -0.5, 0.109375, ((0, 8), (1, 4)))
    out_grad = centred(splits[11], (TOKENS, D), 1.0, 6.0, ((0, 32),))
    routes_keys = jax.random.split(jax.random.fold_in(splits[12], 1), TOKENS // TOK_DEV)
    routes_turns = jax.random.permutation(jax.random.fold_in(splits[12], 3), TOKENS // TOK_DEV)
    routes = jax.vmap(lambda own, number: routed_block(jax.random.fold_in(splits[12], 2), own, number, TOK_DEV, EXPERT_TOTAL, 2, CAP, 1))(routes_keys, routes_turns).reshape((TOKENS, 2))
    segments = draw_segments(jax.random.fold_in(splits[15], 71), 0)
    buckets = draw_buckets(jax.random.fold_in(splits[15], 71), 0)
    return {"tokens": tokens, "w_query": w_query, "w_key": w_key, "w_value": w_value, "w_out_attn": w_out_attn, "w_router": w_router, "gain_attn": gain_attn, "gain_moe": gain_moe, "rel_bias": rel_bias, "w_in": w_in, "w_out": w_out, "out_grad": out_grad, "routes": routes, "segments": segments, "buckets": buckets}


@jax.custom_vjp
def low(v):
    return lax.optimization_barrier(v.astype(jnp.bfloat16)).astype(jnp.float32)

@jax.custom_vjp
def low_back(v):
    return v

def low_keep(v):
    return (low(v), None)

def low_pass(kept, grad):
    return (grad,)

def back_keep(v):
    return (v, None)

def back_low(kept, grad):
    return (low(grad),)
low.defvjp(low_keep, low_pass)
low_back.defvjp(back_keep, back_low)
EPSILON = 1e-06
HIGHEST = lax.Precision.HIGHEST

def rms_norm(values, gain_vector):
    return values * lax.rsqrt(lax.optimization_barrier(jnp.mean(values * values, axis=-1, keepdims=True)) + EPSILON) * gain_vector

def attention(normed, w_query, w_key, w_value, seq_segments, dist_bias):
    seq_length = normed.shape[0]
    head_count = dist_bias.shape[1]
    head_width = normed.shape[1] // head_count
    score_scale = head_width ** (-0.5)
    queries = low(low_back(jnp.dot(normed, w_query, precision=HIGHEST))).reshape(seq_length, head_count, head_width)
    keys_all = low(low_back(jnp.dot(normed, w_key, precision=HIGHEST))).reshape(seq_length, head_count, head_width)
    values_all = low(low_back(jnp.dot(normed, w_value, precision=HIGHEST))).reshape(seq_length, head_count, head_width)
    block_rows = math.gcd(seq_length, 512)
    positions = jnp.arange(seq_length, dtype=jnp.int32)

    def one_block(block_index):
        first_row = block_index * block_rows
        query_block = lax.dynamic_slice_in_dim(queries, first_row, block_rows, 0)
        query_pos = first_row + jnp.arange(block_rows, dtype=jnp.int32)
        query_seg = lax.dynamic_slice_in_dim(seq_segments, first_row, block_rows, 0)
        distance = jnp.clip(query_pos[:, None] - positions[None, :], 0, seq_length - 1)
        bias_values = jnp.transpose(dist_bias[distance], (2, 0, 1))
        scores = jnp.einsum('qhd,khd->hqk', query_block, keys_all, precision=HIGHEST) * score_scale + bias_values
        scores = low_back(scores)
        allowed = (query_pos[:, None] >= positions[None, :]) & (query_seg[:, None] == seq_segments[None, :])
        scores = jnp.where(allowed[None], scores, -1e+30)
        prob_block = low(jax.nn.softmax(scores, axis=-1))
        return jnp.einsum('hqk,khd->qhd', prob_block, values_all, precision=HIGHEST)
    blocks = lax.map(jax.checkpoint(one_block), jnp.arange(seq_length // block_rows, dtype=jnp.int32))
    return blocks.reshape(seq_length, head_count * head_width)

def forward(tokens, w_query, w_key, w_value, w_out_attn, w_router, gain_attn, gain_moe, rel_bias, w_in, w_out, routes, segments, buckets):
    sequences, seq_length = segments.shape
    model_width = tokens.shape[1]
    dist_bias = rel_bias[buckets]

    def one_sequence(seq_pair):
        seq_tokens, seq_segments = seq_pair
        normed = low(rms_norm(seq_tokens, gain_attn))
        mixed_heads = low(low_back(attention(normed, w_query, w_key, w_value, seq_segments, dist_bias)))
        return seq_tokens + low_back(jnp.dot(mixed_heads, w_out_attn, precision=HIGHEST))
    hidden = lax.map(jax.checkpoint(one_sequence), (tokens.reshape(sequences, seq_length, model_width), segments))
    hidden = hidden.reshape(-1, model_width)
    normed = low(rms_norm(hidden, gain_moe))
    logits = low_back(jnp.dot(normed, w_router, precision=HIGHEST))
    router = jax.nn.softmax(logits, axis=-1)
    picked = jnp.take_along_axis(router, routes, axis=1)
    gate_values = picked / lax.optimization_barrier(jnp.sum(picked, axis=1, keepdims=True))
    experts = w_in.shape[0]
    device_list = tokens.shape[0] // TOK_DEV
    flat_routes = routes.reshape(device_list, TOK_DEV * 2)
    onehot = (flat_routes[:, :, None] == jnp.arange(experts, dtype=jnp.int32)[None, None, :]).astype(jnp.int32)
    slot_ranks = lax.optimization_barrier(jnp.sum((jnp.cumsum(onehot, axis=1) - onehot) * onehot, axis=2))
    slot_rows = (jnp.arange(device_list, dtype=jnp.int32)[:, None] * CAP + slot_ranks).reshape(-1, 2).astype(jnp.int32)
    copies = low_back(jnp.broadcast_to(normed[:, None, :], (normed.shape[0], 2, model_width)))
    holding_buffer = jnp.zeros((experts, device_list * CAP, model_width), normed.dtype).at[routes, slot_rows].set(copies)

    def one_expert(triple):
        expert_rows, first_weight, second_weight = triple
        pre_act = low_back(jnp.dot(expert_rows, first_weight, precision=HIGHEST))
        activated = low(jax.nn.gelu(pre_act, approximate=False))
        return low(low_back(jnp.dot(activated, second_weight, precision=HIGHEST)))
    results = lax.map(jax.checkpoint(one_expert), (holding_buffer, w_in, w_out))
    returned = results[routes, slot_rows]
    return hidden + lax.optimization_barrier(jnp.sum(gate_values[:, :, None] * returned, axis=1))

def reference(tokens, w_query, w_key, w_value, w_out_attn, w_router, gain_attn, gain_moe, rel_bias, w_in, w_out, out_grad, routes, segments, buckets):
    floats = [argument.astype(jnp.float32) for argument in (tokens, w_query, w_key, w_value, w_out_attn, w_router, gain_attn, gain_moe, rel_bias, w_in, w_out)]

    def wrapped(*arguments):
        return forward(*arguments, routes, segments, buckets)
    output, pullback = jax.vjp(wrapped, *floats)
    gradients = pullback(out_grad.astype(jnp.float32))
    return (output.astype(jnp.bfloat16), gradients[0].astype(jnp.bfloat16), gradients[1], gradients[2], gradients[3], gradients[4], gradients[5], gradients[6], gradients[7], gradients[8], gradients[9], gradients[10])
```

```python
import math

import jax
import jax.numpy as jnp
from jax import lax
from jax.experimental import pallas as pl
from jax.experimental.pallas import tpu as pltpu
from jax.sharding import PartitionSpec as P

EPSILON = 1e-06
NEG_BIG = -1e30


def matmul(left_operand, right_side):
    return jnp.dot(left_operand, right_side, preferred_element_type=jnp.float32)


def contract_first(left_operand, right_side):
    return lax.dot_general(
        left_operand, right_side, (((0,), (0,)), ((), ())), preferred_element_type=jnp.float32
    )


def contract_last(left_operand, right_side):
    return lax.dot_general(
        left_operand, right_side, (((1,), (1,)), ((), ())), preferred_element_type=jnp.float32
    )


def gelu_slope(pre_act):
    return (
        0.5 * (1.0 + lax.erf(pre_act * 0.7071067811865476))
        + pre_act * jnp.exp(-0.5 * pre_act * pre_act) * 0.3989422804014327
    )


def norm_parts(values, gain_vector):
    inverse = lax.rsqrt(jnp.mean(values * values, axis=-1, keepdims=True) + EPSILON)
    return (values * inverse * gain_vector, inverse)


def norm_back(values, inverse, gain_vector, grad_normed):
    scaled_scores = grad_normed * gain_vector
    grad_gain = jnp.sum(grad_normed * values * inverse, axis=0)
    grad_values = inverse * scaled_scores - values * inverse**3 * jnp.mean(
        scaled_scores * values, axis=-1, keepdims=True
    )
    return (grad_values, grad_gain)


def routed_plan(
    tokens,
    w_query,
    w_key,
    w_value,
    w_out_attn,
    w_router,
    gain_attn,
    gain_moe,
    rel_bias,
    w_in,
    w_out,
    out_grad,
    routes,
    segments,
    buckets,
):
    gathered = (
        lax.all_gather(w_query, "shard", axis=0, tiled=True),
        lax.all_gather(w_key, "shard", axis=0, tiled=True),
        lax.all_gather(w_value, "shard", axis=0, tiled=True),
        lax.all_gather(w_out_attn, "shard", axis=0, tiled=True),
        lax.all_gather(w_router, "shard", axis=0, tiled=True),
        lax.all_gather(gain_attn, "shard", axis=0, tiled=True),
        lax.all_gather(gain_moe, "shard", axis=0, tiled=True),
        lax.all_gather(rel_bias, "shard", axis=0, tiled=True),
    )
    (
        full_query,
        full_key,
        full_value,
        full_proj,
        full_router,
        gain_one,
        gain_two,
        position_bias_table,
    ) = gathered
    expert_first, expert_second = (
        lax.all_gather(w_in, "shard", axis=2, tiled=True),
        lax.all_gather(w_out, "shard", axis=1, tiled=True),
    )
    rows_here, model_width = tokens.shape
    shard_count = lax.axis_size("shard")
    expert_count = lax.axis_size("expert")
    shard_index = lax.axis_index("shard")
    seq_length = rows_here * shard_count
    head_count = position_bias_table.shape[1]
    head_width = model_width // head_count
    score_scale = head_width ** (-0.5)
    local_experts = w_in.shape[0]
    experts = local_experts * expert_count
    capacity = max(2, 4 * rows_here // experts)
    bucket_count = position_bias_table.shape[0]
    gain_one = gain_one.astype(jnp.float32)
    gain_two = gain_two.astype(jnp.float32)
    inputs = tokens.astype(jnp.float32)
    seq_segments = segments[0]
    query_start = shard_index * rows_here
    local_pos = query_start + jnp.arange(rows_here, dtype=jnp.int32)
    local_seg = lax.dynamic_slice_in_dim(seq_segments, query_start, rows_here, 0)
    bucket_ids = jnp.arange(bucket_count, dtype=jnp.int32)
    bucket_starts = jnp.sum((buckets[None, :] < bucket_ids[:, None]).astype(jnp.int32), axis=1)
    bucket_ends = jnp.concatenate([bucket_starts[1:], jnp.full((1,), seq_length, jnp.int32)])

    def bucket_block(query_pos, key_pos):
        distance = jnp.clip(query_pos[:, None] - key_pos[None, :], 0, seq_length - 1)[None]
        inside = (distance >= bucket_starts[:, None, None]) & (
            distance < bucket_ends[:, None, None]
        )
        return inside.astype(jnp.bfloat16)

    normed_one, inverse_one = norm_parts(inputs, gain_one)
    normed_one = normed_one.astype(jnp.bfloat16)
    queries = matmul(normed_one, full_query).astype(jnp.bfloat16)
    keys_here = matmul(normed_one, full_key).astype(jnp.bfloat16)
    values_here = matmul(normed_one, full_value).astype(jnp.bfloat16)
    query_heads = queries.reshape(rows_here, head_count, head_width)
    start_state = (
        jnp.full((head_count, rows_here), NEG_BIG, jnp.float32),
        jnp.zeros((head_count, rows_here), jnp.float32),
        jnp.zeros((rows_here, head_count, head_width), jnp.float32),
    )
    piece_keys = lax.all_gather(keys_here, "shard", axis=0, tiled=True)
    piece_values = lax.all_gather(values_here, "shard", axis=0, tiled=True)
    piece_rows = piece_keys.shape[0]
    block_rows = math.gcd(piece_rows, 512)

    def step(block_index, loop_state):
        running_max, running_sum, accumulated = loop_state
        offset = block_index * block_rows
        key_block = lax.dynamic_slice_in_dim(piece_keys, offset, block_rows, 0).reshape(
            block_rows, head_count, head_width
        )
        value_block = lax.dynamic_slice_in_dim(piece_values, offset, block_rows, 0).reshape(
            block_rows, head_count, head_width
        )
        key_pos = offset + jnp.arange(block_rows, dtype=jnp.int32)
        key_seg = lax.dynamic_slice_in_dim(seq_segments, offset, block_rows, 0)
        distance_bucket_table = bucket_block(local_pos, key_pos)
        bias_values = jnp.einsum(
            "yoc,yi->ioc",
            distance_bucket_table,
            position_bias_table,
            preferred_element_type=jnp.float32,
        )
        allowed = (
            (local_pos[:, None] >= key_pos[None, :]) & (local_seg[:, None] == key_seg[None, :])
        )[None]
        scores = (
            jnp.einsum("qhd,khd->hqk", query_heads, key_block, preferred_element_type=jnp.float32)
            * score_scale
            + bias_values
        )
        scores = jnp.where(allowed, scores, NEG_BIG)
        new_max = jnp.maximum(running_max, jnp.max(scores, axis=2))
        factor = jnp.exp(running_max - new_max)
        prob_block = jnp.where(allowed, jnp.exp(scores - new_max[:, :, None]), 0.0)
        running_sum = running_sum * factor + jnp.sum(prob_block, axis=2)
        accumulated = accumulated * factor.T[:, :, None] + jnp.einsum(
            "hqk,khd->qhd",
            prob_block.astype(jnp.bfloat16),
            value_block,
            preferred_element_type=jnp.float32,
        )
        return (new_max, running_sum, accumulated)

    final_max, final_sum, accumulated = lax.fori_loop(
        0, piece_rows // block_rows, step, start_state
    )
    head_out = accumulated / final_sum.T[:, :, None]
    log_norm = (final_max + jnp.log(final_sum)).T
    mixed_heads = head_out.reshape(rows_here, model_width).astype(jnp.bfloat16)
    hidden = inputs + matmul(mixed_heads, full_proj)
    normed_two, inverse_two = norm_parts(hidden, gain_two)
    normed_two = normed_two.astype(jnp.bfloat16)
    router = jax.nn.softmax(matmul(normed_two, full_router), axis=-1)
    route_onehot = (
        routes[:, :, None] == jnp.arange(experts, dtype=jnp.int32)[None, None, :]
    ).astype(jnp.float32)
    picked = jnp.sum(route_onehot * router[:, None, :], axis=2)
    picked_total = jnp.sum(picked, axis=1, keepdims=True)
    gate_values = picked / picked_total
    flat_routes = routes.reshape(-1)
    flat_onehot = route_onehot.reshape(-1, experts).astype(jnp.int32)
    slot_ranks = jnp.sum((jnp.cumsum(flat_onehot, axis=0) - flat_onehot) * flat_onehot, axis=1)
    doubled = jnp.repeat(normed_two, 2, axis=0)
    outgoing = (
        jnp.zeros((experts, capacity, model_width), jnp.bfloat16)
        .at[flat_routes, slot_ranks]
        .set(doubled)
    )
    arrived = lax.all_to_all(
        outgoing.reshape(expert_count, local_experts * capacity, model_width),
        "expert",
        split_axis=0,
        concat_axis=0,
        tiled=True,
    )
    arrived = arrived.reshape(expert_count, local_experts, capacity, model_width)
    row_list = []
    pre_list = []
    act_list = []
    produced_list = []
    for slot_expert in range(local_experts):
        expert_rows = arrived[:, slot_expert].reshape(expert_count * capacity, model_width)
        pre_act = matmul(expert_rows, expert_first[slot_expert])
        activated = jax.nn.gelu(pre_act, approximate=False).astype(jnp.bfloat16)
        produced = matmul(activated, expert_second[slot_expert]).astype(jnp.bfloat16)
        row_list.append(expert_rows)
        pre_list.append(pre_act)
        act_list.append(activated)
        produced_list.append(produced.reshape(expert_count, 1, capacity, model_width))
    produced_all = jnp.concatenate(produced_list, axis=1).reshape(
        expert_count, local_experts * capacity, model_width
    )
    returned = lax.all_to_all(
        produced_all, "expert", split_axis=0, concat_axis=0, tiled=True
    ).reshape(experts, capacity, model_width)
    route_out = (
        returned[flat_routes, slot_ranks].reshape(rows_here, 2, model_width).astype(jnp.float32)
    )
    layer_out = hidden + jnp.sum(gate_values[:, :, None] * route_out, axis=1)
    grad_final = out_grad.astype(jnp.float32)
    grad_gates = jnp.sum(grad_final[:, None, :] * route_out, axis=2)
    grad_routes = (
        (gate_values[:, :, None] * grad_final[:, None, :])
        .astype(jnp.bfloat16)
        .reshape(-1, model_width)
    )
    grad_outgoing = (
        jnp.zeros((experts, capacity, model_width), jnp.bfloat16)
        .at[flat_routes, slot_ranks]
        .set(grad_routes)
    )
    grad_arrived = lax.all_to_all(
        grad_outgoing.reshape(expert_count, local_experts * capacity, model_width),
        "expert",
        split_axis=0,
        concat_axis=0,
        tiled=True,
    )
    grad_arrived = grad_arrived.reshape(expert_count, local_experts, capacity, model_width)
    grad_in_parts = []
    grad_out_parts = []
    back_list = []
    for slot_expert in range(local_experts):
        grad_rows = grad_arrived[:, slot_expert].reshape(expert_count * capacity, model_width)
        grad_act = contract_last(grad_rows, expert_second[slot_expert])
        grad_pre = (grad_act * gelu_slope(pre_list[slot_expert])).astype(jnp.bfloat16)
        grad_rows_in = contract_last(grad_pre, expert_first[slot_expert]).astype(jnp.bfloat16)
        back_list.append(grad_rows_in.reshape(expert_count, 1, capacity, model_width))
        grad_first = contract_first(row_list[slot_expert], grad_pre)
        grad_second = contract_first(act_list[slot_expert], grad_rows)
        grad_in_parts.append(grad_first)
        grad_out_parts.append(grad_second)
    grad_w_in, grad_w_out = (
        lax.psum_scatter(
            jnp.stack(grad_in_parts).astype(jnp.bfloat16), "shard", scatter_dimension=2, tiled=True
        ).astype(jnp.float32),
        lax.psum_scatter(
            jnp.stack(grad_out_parts).astype(jnp.bfloat16), "shard", scatter_dimension=1, tiled=True
        ).astype(jnp.float32),
    )
    back_all = jnp.concatenate(back_list, axis=1).reshape(
        expert_count, local_experts * capacity, model_width
    )
    sent_back = lax.all_to_all(back_all, "expert", split_axis=0, concat_axis=0, tiled=True).reshape(
        experts, capacity, model_width
    )
    grad_copies = (
        sent_back[flat_routes, slot_ranks].reshape(rows_here, 2, model_width).astype(jnp.float32)
    )
    weighted = jnp.sum(grad_gates * picked, axis=1, keepdims=True)
    grad_picked = grad_gates / picked_total - weighted / (picked_total * picked_total)
    grad_router = jnp.sum(grad_picked[:, :, None] * route_onehot, axis=1)
    grad_logits = (
        router * (grad_router - jnp.sum(router * grad_router, axis=1, keepdims=True))
    ).astype(jnp.bfloat16)
    grad_w_router = contract_first(normed_two, grad_logits)
    grad_normed_two = jnp.sum(grad_copies, axis=1) + contract_last(grad_logits, full_router)
    grad_norm_two, grad_gain_two = norm_back(hidden, inverse_two, gain_two, grad_normed_two)
    grad_hidden = grad_final + grad_norm_two
    grad_branch = grad_hidden.astype(jnp.bfloat16)
    grad_w_proj = contract_first(mixed_heads, grad_branch)
    grad_mixed = contract_last(grad_branch, full_proj).astype(jnp.bfloat16)
    row_dot = jnp.sum(
        grad_mixed.reshape(rows_here, head_count, head_width).astype(jnp.float32) * head_out, axis=2
    )
    all_log_norm, all_row_dot = (
        lax.all_gather(log_norm, "shard", axis=0, tiled=True),
        lax.all_gather(row_dot, "shard", axis=0, tiled=True),
    )
    key_heads = keys_here.reshape(rows_here, head_count, head_width)
    value_heads = values_here.reshape(rows_here, head_count, head_width)
    back_state = (
        jnp.zeros((rows_here, head_count, head_width), jnp.float32),
        jnp.zeros((rows_here, head_count, head_width), jnp.float32),
        jnp.zeros((seq_length, model_width), jnp.float32),
        jnp.zeros((bucket_count, head_count), jnp.float32),
    )
    piece_queries = lax.all_gather(queries, "shard", axis=0, tiled=True)
    piece_grads = lax.all_gather(grad_mixed, "shard", axis=0, tiled=True)
    piece_rows = piece_queries.shape[0]
    attend_block_rows = math.gcd(piece_rows, 512)

    def step(block_index, loop_state):
        grad_keys, grad_values, grad_queries, grad_bias = loop_state
        offset = block_index * attend_block_rows
        query_block = lax.dynamic_slice_in_dim(piece_queries, offset, attend_block_rows, 0).reshape(
            attend_block_rows, head_count, head_width
        )
        grad_block = lax.dynamic_slice_in_dim(piece_grads, offset, attend_block_rows, 0).reshape(
            attend_block_rows, head_count, head_width
        )
        query_pos = offset + jnp.arange(attend_block_rows, dtype=jnp.int32)
        query_seg = lax.dynamic_slice_in_dim(seq_segments, offset, attend_block_rows, 0)
        norm_block = lax.dynamic_slice_in_dim(all_log_norm, offset, attend_block_rows, 0)
        dot_block = lax.dynamic_slice_in_dim(all_row_dot, offset, attend_block_rows, 0)
        distance_bucket_table = bucket_block(query_pos, local_pos)
        bias_values = jnp.einsum(
            "yoc,yi->ioc",
            distance_bucket_table,
            position_bias_table,
            preferred_element_type=jnp.float32,
        )
        allowed = (
            (query_pos[:, None] >= local_pos[None, :]) & (query_seg[:, None] == local_seg[None, :])
        )[None]
        scores = (
            jnp.einsum("qhd,khd->hqk", query_block, key_heads, preferred_element_type=jnp.float32)
            * score_scale
            + bias_values
        )
        prob_block = jnp.where(allowed, jnp.exp(scores - norm_block.T[:, :, None]), 0.0)
        grad_values = grad_values + jnp.einsum(
            "hqk,qhd->khd",
            prob_block.astype(jnp.bfloat16),
            grad_block,
            preferred_element_type=jnp.float32,
        )
        grad_probs = jnp.einsum(
            "qhd,khd->hqk", grad_block, value_heads, preferred_element_type=jnp.float32
        )
        score_gradient = (prob_block * (grad_probs - dot_block.T[:, :, None])).astype(jnp.bfloat16)
        grad_keys = (
            grad_keys
            + jnp.einsum(
                "hqk,qhd->khd", score_gradient, query_block, preferred_element_type=jnp.float32
            )
            * score_scale
        )
        query_part = (
            jnp.einsum(
                "hqk,khd->qhd", score_gradient, key_heads, preferred_element_type=jnp.float32
            )
            * score_scale
        )
        grad_queries = lax.dynamic_update_slice_in_dim(
            grad_queries, query_part.reshape(attend_block_rows, model_width), offset, 0
        )
        grad_bias = grad_bias + jnp.einsum(
            "iof,mof->mi", score_gradient, distance_bucket_table, preferred_element_type=jnp.float32
        )
        return (grad_keys, grad_values, grad_queries, grad_bias)

    grad_keys, grad_values, grad_queries, grad_bias_table = lax.fori_loop(
        0, piece_rows // attend_block_rows, step, back_state
    )
    grad_query_here = lax.psum_scatter(
        grad_queries.astype(jnp.bfloat16), "shard", scatter_dimension=0, tiled=True
    )
    grad_key_here = grad_keys.reshape(rows_here, model_width).astype(jnp.bfloat16)
    grad_value_here = grad_values.reshape(rows_here, model_width).astype(jnp.bfloat16)
    grad_w_query = contract_first(normed_one, grad_query_here)
    grad_w_key = contract_first(normed_one, grad_key_here)
    grad_w_value = contract_first(normed_one, grad_value_here)
    grad_normed_one = (
        contract_last(grad_query_here, full_query)
        + contract_last(grad_key_here, full_key)
        + contract_last(grad_value_here, full_value)
    )
    grad_norm_one, grad_gain_one = norm_back(inputs, inverse_one, gain_one, grad_normed_one)
    tokens_grad = (grad_hidden + grad_norm_one).astype(jnp.bfloat16)
    shares = (
        lax.psum_scatter(
            grad_w_query.astype(jnp.bfloat16), "shard", scatter_dimension=0, tiled=True
        ).astype(jnp.float32),
        lax.psum_scatter(
            grad_w_key.astype(jnp.bfloat16), "shard", scatter_dimension=0, tiled=True
        ).astype(jnp.float32),
        lax.psum_scatter(
            grad_w_value.astype(jnp.bfloat16), "shard", scatter_dimension=0, tiled=True
        ).astype(jnp.float32),
        lax.psum_scatter(
            grad_w_proj.astype(jnp.bfloat16), "shard", scatter_dimension=0, tiled=True
        ).astype(jnp.float32),
        lax.psum_scatter(
            grad_w_router.astype(jnp.bfloat16), "shard", scatter_dimension=0, tiled=True
        ).astype(jnp.float32),
        lax.psum_scatter(
            grad_gain_one.astype(jnp.bfloat16), "shard", scatter_dimension=0, tiled=True
        ).astype(jnp.float32),
        lax.psum_scatter(
            grad_gain_two.astype(jnp.bfloat16), "shard", scatter_dimension=0, tiled=True
        ).astype(jnp.float32),
        lax.psum_scatter(
            grad_bias_table.astype(jnp.bfloat16), "shard", scatter_dimension=0, tiled=True
        ).astype(jnp.float32),
    )
    totals = (
        lax.psum(shares[0].astype(jnp.bfloat16), "expert").astype(jnp.float32),
        lax.psum(shares[1].astype(jnp.bfloat16), "expert").astype(jnp.float32),
        lax.psum(shares[2].astype(jnp.bfloat16), "expert").astype(jnp.float32),
        lax.psum(shares[3].astype(jnp.bfloat16), "expert").astype(jnp.float32),
        lax.psum(shares[4].astype(jnp.bfloat16), "expert").astype(jnp.float32),
        lax.psum(shares[5].astype(jnp.bfloat16), "expert").astype(jnp.float32),
        lax.psum(shares[6].astype(jnp.bfloat16), "expert").astype(jnp.float32),
        lax.psum(shares[7].astype(jnp.bfloat16), "expert").astype(jnp.float32),
    )
    return (
        layer_out.astype(jnp.bfloat16),
        tokens_grad,
        totals[0],
        totals[1],
        totals[2],
        totals[3],
        totals[4],
        totals[5],
        totals[6],
        totals[7],
        grad_w_in,
        grad_w_out,
    )


VMEM_BYTES = 60 * 1024 * 1024
TILE = 256
PACK_ROWS = 16
DENSE_TOKENS = 16384


def attend_forward(qkv_ref, skew_ref, seg_col_ref, seg_row_ref, out_ref, prob_ref, toeplitz):
    heads, seq_length = prob_ref.shape[0], prob_ref.shape[1]
    width = out_ref.shape[1] // heads
    tiles = seq_length // TILE
    scale = width ** (-0.5)
    lower = lax.broadcasted_iota(jnp.int32, (TILE, TILE), 0) >= lax.broadcasted_iota(
        jnp.int32, (TILE, TILE), 1
    )
    for head in range(heads):
        for delta in range(tiles):
            row = skew_ref[head, delta : delta + 1, :]
            wide = jnp.broadcast_to(row, (TILE, 2 * TILE))
            turned = pltpu.roll(wide, 0, 1, stride=1, stride_axis=0)[:, :TILE]
            if delta == 0:
                turned = jnp.where(lower, turned, NEG_BIG)
            toeplitz[delta] = turned
        query_cols = pl.ds(head * width, width)
        key_cols = pl.ds((heads + head) * width, width)
        value_cols = pl.ds((2 * heads + head) * width, width)
        for tile in range(tiles):
            rows = pl.ds(tile * TILE, TILE)
            extent = (tile + 1) * TILE
            query = qkv_ref[rows, query_cols]
            scores = contract_last(query, qkv_ref[pl.ds(0, extent), key_cols]) * scale
            bias = jnp.concatenate([toeplitz[tile - other] for other in range(tile + 1)], axis=1)
            same = seg_col_ref[rows, :] == seg_row_ref[:, pl.ds(0, extent)]
            scores = jnp.where(same, scores + bias, NEG_BIG)
            top = jnp.max(scores, axis=1, keepdims=True)
            weight = jnp.exp(scores - top)
            total = jnp.sum(weight, axis=1, keepdims=True)
            prob = (weight * (1.0 / total)).astype(jnp.bfloat16)
            prob_ref[head, rows, pl.ds(0, extent)] = prob
            out_ref[rows, query_cols] = matmul(
                prob, qkv_ref[pl.ds(0, extent), value_cols]
            ).astype(jnp.bfloat16)


def attend_backward(qkv_ref, grad_ref, prob_ref, grad_qkv_ref, diag_ref, keys_acc, values_acc, blocks):
    heads, seq_length = prob_ref.shape[0], prob_ref.shape[1]
    width = grad_ref.shape[1] // heads
    tiles = seq_length // TILE
    scale = width ** (-0.5)
    flip = (
        lax.broadcasted_iota(jnp.int32, (TILE, TILE), 0)
        + lax.broadcasted_iota(jnp.int32, (TILE, TILE), 1)
        == TILE - 1
    ).astype(jnp.float32)
    for head in range(heads):
        query_cols = pl.ds(head * width, width)
        key_cols = pl.ds((heads + head) * width, width)
        value_cols = pl.ds((2 * heads + head) * width, width)
        keys_acc[...] = jnp.zeros_like(keys_acc)
        values_acc[...] = jnp.zeros_like(values_acc)
        blocks[...] = jnp.zeros_like(blocks)
        for tile in range(tiles):
            rows = pl.ds(tile * TILE, TILE)
            extent = (tile + 1) * TILE
            seen = pl.ds(0, extent)
            query = qkv_ref[rows, query_cols]
            grad = grad_ref[rows, query_cols]
            prob = prob_ref[head, rows, seen]
            wide = prob.astype(jnp.float32)
            grad_prob = contract_last(grad, qkv_ref[seen, value_cols])
            dots = jnp.sum(wide * grad_prob, axis=1, keepdims=True)
            grad_score = (wide * (grad_prob - dots)).astype(jnp.bfloat16)
            grad_qkv_ref[rows, query_cols] = (
                matmul(grad_score, qkv_ref[seen, key_cols]) * scale
            ).astype(jnp.bfloat16)
            keys_acc[seen, :] += contract_first(grad_score, query)
            values_acc[seen, :] += contract_first(prob, grad)
            for other in range(tile + 1):
                blocks[tile - other] += grad_score[:, other * TILE : (other + 1) * TILE].astype(
                    jnp.float32
                )
        grad_qkv_ref[:, key_cols] = (keys_acc[...] * scale).astype(jnp.bfloat16)
        grad_qkv_ref[:, value_cols] = values_acc[...].astype(jnp.bfloat16)
        for delta in range(tiles):
            flipped = jnp.dot(
                flip,
                blocks[delta],
                precision=lax.Precision.HIGHEST,
                preferred_element_type=jnp.float32,
            )
            padded = jnp.concatenate([flipped, jnp.zeros_like(flipped)], axis=1)
            turned = pltpu.roll(padded, 0, 1, stride=1, stride_axis=0)
            diag_ref[head, delta : delta + 1, :] = jnp.sum(turned, axis=0, keepdims=True)


def expert_step(
    ranks_ref,
    gates_ref,
    rows_ref,
    grads_ref,
    first_ref,
    second_ref,
    out_ref,
    back_ref,
    dots_ref,
    grad_first_ref,
    grad_second_ref,
):
    local_experts, group, _, block = ranks_ref.shape
    capacity = 64 * block // 256

    @pl.when(pl.program_id(0) == 0)
    def _():
        grad_first_ref[...] = jnp.zeros_like(grad_first_ref)
        grad_second_ref[...] = jnp.zeros_like(grad_second_ref)

    slot = lax.broadcasted_iota(jnp.int32, (capacity, block), 0).astype(jnp.float32)
    for expert in range(local_experts):
        picks = [ranks_ref[expert, at] == slot for at in range(group)]
        ones = [pick.astype(jnp.float32).astype(jnp.bfloat16) for pick in picks]
        gate = jnp.concatenate(
            [
                jnp.sum(jnp.where(picks[at], gates_ref[expert, at], 0.0), axis=1, keepdims=True)
                for at in range(group)
            ],
            axis=0,
        )
        rows = jnp.concatenate(
            [matmul(ones[at], rows_ref[at]).astype(jnp.bfloat16) for at in range(group)], axis=0
        )
        grads = jnp.concatenate(
            [matmul(ones[at], grads_ref[at, pl.ds(0, block), :]) for at in range(group)], axis=0
        )
        pre = matmul(rows, first_ref[expert])
        half = 0.5 * (1.0 + lax.erf(pre * 0.7071067811865476))
        act = (pre * half).astype(jnp.bfloat16)
        slope = half + pre * jnp.exp(-0.5 * pre * pre) * 0.3989422804014327
        produced = matmul(act, second_ref[expert])
        dots = jnp.sum(grads * produced, axis=1, keepdims=True)
        given = (gate * grads).astype(jnp.bfloat16)
        weighted = (gate * produced).astype(jnp.bfloat16)
        grad_pre = (contract_last(given, second_ref[expert]) * slope).astype(jnp.bfloat16)
        back = contract_last(grad_pre, first_ref[expert]).astype(jnp.bfloat16)
        grad_first_ref[expert] += contract_first(rows, grad_pre)
        grad_second_ref[expert] += contract_first(act, given)
        for at in range(group):
            part = slice(at * capacity, (at + 1) * capacity)
            out_part = contract_first(ones[at], weighted[part])
            back_part = contract_first(ones[at], back[part])
            if expert > 0:
                out_part = out_part + out_ref[at].astype(jnp.float32)
                back_part = back_part + back_ref[at].astype(jnp.float32)
            out_ref[at] = out_part.astype(jnp.bfloat16)
            back_ref[at] = back_part.astype(jnp.bfloat16)
            dots_ref[expert, at] = jnp.sum(
                jnp.where(picks[at], dots[part], 0.0), axis=0, keepdims=True
            )


def run_experts(ranks, gates, rows, grads, first, second):
    local_experts, blocks, _, block = ranks.shape
    width = rows.shape[2]
    group = math.gcd(blocks, 4)
    small = pl.BlockSpec((local_experts, group, 1, block), lambda i: (0, i, 0, 0))
    fixed = lambda shape: pl.BlockSpec(
        shape, lambda i: (0, 0, 0), pipeline_mode=pl.Buffered(1)
    )
    tall = pl.BlockSpec((group, block, width), lambda i: (i, 0, 0))
    return pl.pallas_call(
        expert_step,
        grid=(blocks // group,),
        in_specs=[
            small,
            small,
            tall,
            pl.BlockSpec((group, grads.shape[1], width), lambda i: (i, 0, 0)),
            fixed(first.shape),
            fixed(second.shape),
        ],
        out_specs=[tall, tall, small, fixed(first.shape), fixed(second.shape)],
        out_shape=[
            jax.ShapeDtypeStruct((blocks, block, width), jnp.bfloat16),
            jax.ShapeDtypeStruct((blocks, block, width), jnp.bfloat16),
            jax.ShapeDtypeStruct(ranks.shape, jnp.float32),
            jax.ShapeDtypeStruct(first.shape, jnp.float32),
            jax.ShapeDtypeStruct(second.shape, jnp.float32),
        ],
        compiler_params=pltpu.CompilerParams(vmem_limit_bytes=VMEM_BYTES),
    )(ranks, gates, rows, grads, first, second)


def pad_rows(flat, rows, width):
    return jnp.concatenate(
        [flat, jnp.zeros((rows * width - flat.shape[0],), flat.dtype)]
    ).reshape(rows, width)


def dense_plan(
    tokens,
    w_query,
    w_key,
    w_value,
    w_out_attn,
    w_router,
    gain_attn,
    gain_moe,
    rel_bias,
    w_in,
    w_out,
    out_grad,
    routes,
    segments,
    buckets,
):
    block, width = tokens.shape
    shards = lax.axis_size("shard")
    groups = lax.axis_size("expert")
    seq_length = block * shards
    head_count = rel_bias.shape[1]
    heads = head_count // shards
    head_width = width // head_count
    owned = heads * head_width
    experts = w_router.shape[1]
    local_experts = w_in.shape[0]
    bucket_count = rel_bias.shape[0] * shards
    part_rows = w_router.shape[0]
    blocks = groups * shards
    tiles = seq_length // TILE
    shard_at = lax.axis_index("shard")
    expert_at = lax.axis_index("expert")
    bf16, f32 = jnp.bfloat16, jnp.float32

    small = jnp.concatenate(
        [w_router.reshape(-1), gain_attn.reshape(-1), gain_moe.reshape(-1), rel_bias.reshape(-1)]
    )
    opening = jnp.concatenate([tokens, pad_rows(small, PACK_ROWS, width)], axis=0)
    opened = lax.all_gather(opening, "shard", axis=0)
    tokens_seq = opened[:, :block].reshape(seq_length, width)
    smalls = opened[:, block:].reshape(shards, -1)
    at = part_rows * experts
    full_router = smalls[:, :at].reshape(width, experts)
    gain_one = smalls[:, at : at + part_rows].reshape(width).astype(f32)
    gain_two = smalls[:, at + part_rows : at + 2 * part_rows].reshape(width).astype(f32)
    at = at + 2 * part_rows
    table = smalls[:, at : at + rel_bias.size].reshape(bucket_count, head_count)

    stacked = jnp.stack([w_query, w_key, w_value], axis=1).reshape(part_rows, 3, shards, owned)
    stacked = stacked.transpose(2, 0, 1, 3).reshape(shards, part_rows, 3 * owned)
    own_qkv = lax.all_to_all(stacked, "shard", split_axis=0, concat_axis=0, tiled=True)
    own_qkv = own_qkv.reshape(width, 3 * owned)
    full_proj = lax.all_gather(w_out_attn, "shard", axis=0, tiled=True)

    closing = jnp.concatenate(
        [out_grad, pad_rows(routes.T.reshape(-1).astype(bf16), PACK_ROWS, width)], axis=0
    )
    closed = lax.all_gather(closing, ("expert", "shard"), axis=0)

    inputs_seq = tokens_seq.astype(f32)
    normed_seq, inverse_seq = norm_parts(inputs_seq, gain_one)
    normed_seq = normed_seq.astype(bf16)
    qkv = matmul(normed_seq, own_qkv).astype(bf16)
    bucket_hot = (buckets[:, None] == jnp.arange(bucket_count, dtype=jnp.int32)[None, :]).astype(bf16)
    own_table = lax.dynamic_slice_in_dim(table, shard_at * heads, heads, 1)
    by_distance = lax.dot_general(
        own_table, bucket_hot, (((0,), (1,)), ((), ())), preferred_element_type=f32
    )
    descending = jnp.pad(by_distance, ((0, 0), (TILE, TILE)))[:, ::-1]
    pieces = []
    for delta in range(tiles):
        low_at = seq_length + TILE - 1 - delta * TILE
        pieces.append(
            jnp.concatenate(
                [descending[:, low_at : low_at + TILE], descending[:, low_at - TILE : low_at]], axis=1
            )
        )
    skew = jnp.stack(pieces, axis=1)
    seg = segments[0]
    mixed, prob = pl.pallas_call(
        attend_forward,
        out_shape=[
            jax.ShapeDtypeStruct((seq_length, owned), bf16),
            jax.ShapeDtypeStruct((heads, seq_length, seq_length), bf16),
        ],
        scratch_shapes=[pltpu.VMEM((tiles, TILE, TILE), f32)],
        compiler_params=pltpu.CompilerParams(vmem_limit_bytes=VMEM_BYTES),
    )(qkv, skew, seg[:, None], seg[None, :])
    mixed_here = lax.all_to_all(
        mixed.reshape(shards, block, owned), "shard", split_axis=0, concat_axis=0, tiled=True
    )
    mixed_here = mixed_here.transpose(1, 0, 2).reshape(block, width)

    inputs = tokens.astype(f32)
    hidden = inputs + matmul(mixed_here, full_proj)
    normed_two, inverse_two = norm_parts(hidden, gain_two)
    normed_two = normed_two.astype(bf16)
    normed_all = lax.all_gather(normed_two, ("expert", "shard"), axis=0)
    expert_ids = jnp.arange(experts, dtype=jnp.int32)

    grads_all = closed
    routes_all = closed[:, block].reshape(blocks, width)[:, : 2 * block]
    routes_all = routes_all.reshape(blocks, 2, block).astype(jnp.int32)
    logits_all = lax.dot_general(
        full_router, normed_all, (((0,), (2,)), ((), ())), preferred_element_type=f32
    )
    router_all = jax.nn.softmax(logits_all, axis=0)
    own_ids = expert_at * local_experts + jnp.arange(local_experts, dtype=jnp.int32)
    named = (routes_all[None] == own_ids[:, None, None, None]).any(axis=2)
    first_hot = routes_all[None, :, 0] == expert_ids[:, None, None]
    second_hot = routes_all[None, :, 1] == expert_ids[:, None, None]
    picked_sum = jnp.sum(jnp.where(first_hot | second_hot, router_all, 0.0), axis=0)
    own_router = lax.dynamic_slice_in_dim(router_all, expert_at * local_experts, local_experts, 0)
    gates_all = jnp.where(named, own_router / picked_sum[None], 0.0)
    before = (jnp.arange(block)[:, None] < jnp.arange(block)[None, :]).astype(bf16)
    ranks = matmul(named.astype(bf16).reshape(-1, block), before).reshape(named.shape)
    ranks = jnp.where(named, ranks, -1.0)
    out_parts, back_parts, dots, grad_w_in, grad_w_out = run_experts(
        ranks[:, :, None, :], gates_all[:, :, None, :], normed_all, grads_all, w_in, w_out
    )
    dots = dots[:, :, 0, :]
    dots_by_choice = jnp.sum(
        jnp.where(routes_all[None] == own_ids[:, None, None, None], dots[:, :, None, :], 0.0), axis=0
    )
    dots_rows = jnp.pad(
        dots_by_choice.astype(bf16).reshape(blocks, 1, 2 * block),
        ((0, 0), (0, PACK_ROWS - 1), (0, width - 2 * block)),
    )
    back_parts = jnp.concatenate([back_parts, dots_rows], axis=1)
    back_here = lax.psum_scatter(back_parts, ("expert", "shard"), scatter_dimension=0, tiled=True)[0]
    out_here = lax.psum_scatter(out_parts, ("expert", "shard"), scatter_dimension=0, tiled=True)[0]
    layer_out = (hidden + out_here.astype(f32)).astype(bf16)

    router = jax.nn.softmax(matmul(normed_two, full_router), axis=-1)
    route_onehot = (routes[:, :, None] == expert_ids[None, None, :]).astype(f32)
    picked = jnp.sum(route_onehot * router[:, None, :], axis=2)
    picked_total = jnp.sum(picked, axis=1, keepdims=True)
    grad_gates = back_here[block, : 2 * block].reshape(2, block).T.astype(f32)
    weighted = jnp.sum(grad_gates * picked, axis=1, keepdims=True)
    grad_picked = grad_gates / picked_total - weighted / (picked_total * picked_total)
    grad_router = jnp.sum(grad_picked[:, :, None] * route_onehot, axis=1)
    grad_logits = (
        router * (grad_router - jnp.sum(router * grad_router, axis=1, keepdims=True))
    ).astype(bf16)
    grad_w_router = contract_first(normed_two, grad_logits)
    grad_normed_two = back_here[:block].astype(f32) + contract_last(grad_logits, full_router)
    grad_norm_two, grad_gain_two = norm_back(hidden, inverse_two, gain_two, grad_normed_two)
    grad_hidden = out_grad.astype(f32) + grad_norm_two
    grad_branch = lax.all_gather(grad_hidden.astype(bf16), "shard", axis=0, tiled=True)

    grad_w_proj = contract_first(mixed, grad_branch)
    grad_mixed = contract_last(grad_branch, w_out_attn).astype(bf16)
    grad_qkv, diagonals = pl.pallas_call(
        attend_backward,
        out_shape=[
            jax.ShapeDtypeStruct((seq_length, 3 * owned), bf16),
            jax.ShapeDtypeStruct((heads, tiles, 2 * TILE), f32),
        ],
        scratch_shapes=[
            pltpu.VMEM((seq_length, head_width), f32),
            pltpu.VMEM((seq_length, head_width), f32),
            pltpu.VMEM((tiles, TILE, TILE), f32),
        ],
        compiler_params=pltpu.CompilerParams(vmem_limit_bytes=VMEM_BYTES),
    )(qkv, grad_mixed, prob)
    grad_normed_one = contract_last(grad_qkv, own_qkv)
    norm_one_here = lax.psum_scatter(
        grad_normed_one.astype(bf16), "shard", scatter_dimension=0, tiled=True
    ).astype(f32)
    grad_gain_one = jnp.sum(grad_normed_one * inputs_seq * inverse_seq, axis=0)
    by_distance_grad = jnp.zeros((heads, seq_length + TILE), f32)
    for delta in range(tiles):
        piece = diagonals[:, delta, ::-1]
        start = delta * TILE
        by_distance_grad = by_distance_grad.at[:, start : start + 2 * TILE].add(piece)
    by_distance_grad = by_distance_grad[:, TILE : TILE + seq_length]
    grad_table = lax.dot_general(
        bucket_hot.astype(f32),
        by_distance_grad,
        (((0,), (1,)), ((), ())),
        precision=lax.Precision.HIGHEST,
        preferred_element_type=f32,
    )
    grad_qkv_full = contract_first(normed_seq, grad_qkv)

    bias_rows = grad_table.reshape(shards, -1)
    tail = jnp.concatenate(
        [
            grad_w_router.reshape(shards, -1),
            grad_gain_one.reshape(shards, -1),
            grad_gain_two.reshape(shards, -1),
            bias_rows,
        ],
        axis=1,
    )
    tail_rows = -(-tail.shape[1] // (3 * owned))
    tail_rows = -(-tail_rows // 16) * 16
    tail = jnp.pad(tail, ((0, 0), (0, tail_rows * 3 * owned - tail.shape[1])))
    leaving = jnp.concatenate(
        [
            grad_qkv_full.reshape(shards, part_rows, 3 * owned),
            tail.reshape(shards, tail_rows, 3 * owned),
        ],
        axis=1,
    ).astype(bf16)
    landed = lax.all_to_all(leaving, "shard", split_axis=0, concat_axis=0, tiled=True)
    landed_tail = landed[:, part_rows:].reshape(shards, -1)
    plain = part_rows * (experts + 2)
    summed_tail = jnp.sum(landed_tail[:, :plain].astype(f32), axis=0).astype(bf16)
    bias_count = rel_bias.shape[0] * heads
    final = jnp.concatenate(
        [
            landed[:, :part_rows].reshape(-1),
            grad_w_proj.astype(bf16).reshape(-1),
            summed_tail,
            landed_tail[:, plain : plain + bias_count].reshape(-1),
        ]
    )
    length = final.shape[0]
    final = jnp.pad(final, (0, -length % 2048)).reshape(-1, 128)
    final = lax.psum(final, "expert").reshape(-1).astype(f32)
    size = part_rows * width
    grads_qkv = final[: 3 * size].reshape(shards, part_rows, 3, owned)
    grads_qkv = grads_qkv.transpose(2, 1, 0, 3).reshape(3, part_rows, width)
    proj_total = final[3 * size : 4 * size].reshape(part_rows, width)
    rest = final[4 * size : length]
    router_total = rest[: part_rows * experts].reshape(part_rows, experts)
    gain_one_total = rest[part_rows * experts : part_rows * (experts + 1)]
    gain_two_total = rest[part_rows * (experts + 1) : plain]
    bias_total = rest[plain:].reshape(shards, rel_bias.shape[0], heads)
    bias_total = bias_total.transpose(1, 0, 2).reshape(rel_bias.shape)

    inverse_one = lax.rsqrt(jnp.mean(inputs * inputs, axis=-1, keepdims=True) + EPSILON)
    grad_norm_one, _ = norm_back(inputs, inverse_one, gain_one, norm_one_here)
    tokens_grad = (grad_hidden + grad_norm_one).astype(bf16)
    return (
        layer_out,
        tokens_grad,
        grads_qkv[0],
        grads_qkv[1],
        grads_qkv[2],
        proj_total,
        router_total,
        gain_one_total,
        gain_two_total,
        bias_total,
        grad_w_in,
        grad_w_out,
    )


def per_device(*arguments):
    tokens, rel_bias = arguments[0], arguments[8]
    shards = lax.axis_size("shard")
    every = tokens.shape[0] * shards * lax.axis_size("expert")
    if every > DENSE_TOKENS or rel_bias.shape[1] % shards or tokens.shape[0] % TILE:
        return routed_plan(*arguments)
    return dense_plan(*arguments)


def solution(mesh):
    placed = (
        P(("expert", "shard"), None),
        P("shard", None),
        P("shard", None),
        P("shard", None),
        P("shard", None),
        P("shard", None),
        P("shard"),
        P("shard"),
        P("shard", None),
        P("expert", None, "shard"),
        P("expert", "shard", None),
        P(("expert", "shard"), None),
        P(("expert", "shard"), None),
        P("expert", None),
        P(),
    )
    return jax.shard_map(
        per_device,
        mesh=mesh,
        in_specs=placed,
        out_specs=(
            P(("expert", "shard"), None),
            P(("expert", "shard"), None),
            P("shard", None),
            P("shard", None),
            P("shard", None),
            P("shard", None),
            P("shard", None),
            P("shard"),
            P("shard"),
            P("shard", None),
            P("expert", None, "shard"),
            P("expert", "shard", None),
        ),
        check_vma=False,
    )
```

```python
import math

import jax
import jax.numpy as jnp
from jax import lax
from jax.experimental import pallas as pl
from jax.experimental.pallas import tpu as pltpu
from jax.sharding import PartitionSpec as P

EPSILON = 1e-06
NEG_BIG = -1e30


def matmul(left_operand, right_side):
    return jnp.dot(left_operand, right_side, preferred_element_type=jnp.float32)


def contract_first(left_operand, right_side):
    return lax.dot_general(
        left_operand, right_side, (((0,), (0,)), ((), ())), preferred_element_type=jnp.float32
    )


def contract_last(left_operand, right_side):
    return lax.dot_general(
        left_operand, right_side, (((1,), (1,)), ((), ())), preferred_element_type=jnp.float32
    )


def gelu_slope(pre_act):
    return (
        0.5 * (1.0 + lax.erf(pre_act * 0.7071067811865476))
        + pre_act * jnp.exp(-0.5 * pre_act * pre_act) * 0.3989422804014327
    )


def norm_parts(values, gain_vector):
    inverse = lax.rsqrt(jnp.mean(values * values, axis=-1, keepdims=True) + EPSILON)
    return (values * inverse * gain_vector, inverse)


def norm_back(values, inverse, gain_vector, grad_normed):
    scaled_scores = grad_normed * gain_vector
    grad_gain = jnp.sum(grad_normed * values * inverse, axis=0)
    grad_values = inverse * scaled_scores - values * inverse**3 * jnp.mean(
        scaled_scores * values, axis=-1, keepdims=True
    )
    return (grad_values, grad_gain)


def routed_plan(
    tokens,
    w_query,
    w_key,
    w_value,
    w_out_attn,
    w_router,
    gain_attn,
    gain_moe,
    rel_bias,
    w_in,
    w_out,
    out_grad,
    routes,
    segments,
    buckets,
):
    gathered = (
        lax.all_gather(w_query, "shard", axis=0, tiled=True),
        lax.all_gather(w_key, "shard", axis=0, tiled=True),
        lax.all_gather(w_value, "shard", axis=0, tiled=True),
        lax.all_gather(w_out_attn, "shard", axis=0, tiled=True),
        lax.all_gather(w_router, "shard", axis=0, tiled=True),
        lax.all_gather(gain_attn, "shard", axis=0, tiled=True),
        lax.all_gather(gain_moe, "shard", axis=0, tiled=True),
        lax.all_gather(rel_bias, "shard", axis=0, tiled=True),
    )
    (
        full_query,
        full_key,
        full_value,
        full_proj,
        full_router,
        gain_one,
        gain_two,
        position_bias_table,
    ) = gathered
    expert_first, expert_second = (
        lax.all_gather(w_in, "shard", axis=2, tiled=True),
        lax.all_gather(w_out, "shard", axis=1, tiled=True),
    )
    rows_here, model_width = tokens.shape
    shard_count = lax.axis_size("shard")
    expert_count = lax.axis_size("expert")
    shard_index = lax.axis_index("shard")
    seq_length = rows_here * shard_count
    head_count = position_bias_table.shape[1]
    head_width = model_width // head_count
    score_scale = head_width ** (-0.5)
    local_experts = w_in.shape[0]
    experts = local_experts * expert_count
    capacity = max(2, 4 * rows_here // experts)
    bucket_count = position_bias_table.shape[0]
    gain_one = gain_one.astype(jnp.float32)
    gain_two = gain_two.astype(jnp.float32)
    inputs = tokens.astype(jnp.float32)
    seq_segments = segments[0]
    query_start = shard_index * rows_here
    local_pos = query_start + jnp.arange(rows_here, dtype=jnp.int32)
    local_seg = lax.dynamic_slice_in_dim(seq_segments, query_start, rows_here, 0)
    bucket_ids = jnp.arange(bucket_count, dtype=jnp.int32)
    bucket_starts = jnp.sum((buckets[None, :] < bucket_ids[:, None]).astype(jnp.int32), axis=1)
    bucket_ends = jnp.concatenate([bucket_starts[1:], jnp.full((1,), seq_length, jnp.int32)])

    def bucket_block(query_pos, key_pos):
        distance = jnp.clip(query_pos[:, None] - key_pos[None, :], 0, seq_length - 1)[None]
        inside = (distance >= bucket_starts[:, None, None]) & (
            distance < bucket_ends[:, None, None]
        )
        return inside.astype(jnp.bfloat16)

    normed_one, inverse_one = norm_parts(inputs, gain_one)
    normed_one = normed_one.astype(jnp.bfloat16)
    queries = matmul(normed_one, full_query).astype(jnp.bfloat16)
    keys_here = matmul(normed_one, full_key).astype(jnp.bfloat16)
    values_here = matmul(normed_one, full_value).astype(jnp.bfloat16)
    query_heads = queries.reshape(rows_here, head_count, head_width)
    start_state = (
        jnp.full((head_count, rows_here), NEG_BIG, jnp.float32),
        jnp.zeros((head_count, rows_here), jnp.float32),
        jnp.zeros((rows_here, head_count, head_width), jnp.float32),
    )
    piece_keys = lax.all_gather(keys_here, "shard", axis=0, tiled=True)
    piece_values = lax.all_gather(values_here, "shard", axis=0, tiled=True)
    piece_rows = piece_keys.shape[0]
    block_rows = math.gcd(piece_rows, 512)

    def step(block_index, loop_state):
        running_max, running_sum, accumulated = loop_state
        offset = block_index * block_rows
        key_block = lax.dynamic_slice_in_dim(piece_keys, offset, block_rows, 0).reshape(
            block_rows, head_count, head_width
        )
        value_block = lax.dynamic_slice_in_dim(piece_values, offset, block_rows, 0).reshape(
            block_rows, head_count, head_width
        )
        key_pos = offset + jnp.arange(block_rows, dtype=jnp.int32)
        key_seg = lax.dynamic_slice_in_dim(seq_segments, offset, block_rows, 0)
        distance_bucket_table = bucket_block(local_pos, key_pos)
        bias_values = jnp.einsum(
            "yoc,yi->ioc",
            distance_bucket_table,
            position_bias_table,
            preferred_element_type=jnp.float32,
        )
        allowed = (
            (local_pos[:, None] >= key_pos[None, :]) & (local_seg[:, None] == key_seg[None, :])
        )[None]
        scores = (
            jnp.einsum("qhd,khd->hqk", query_heads, key_block, preferred_element_type=jnp.float32)
            * score_scale
            + bias_values
        )
        scores = jnp.where(allowed, scores, NEG_BIG)
        new_max = jnp.maximum(running_max, jnp.max(scores, axis=2))
        factor = jnp.exp(running_max - new_max)
        prob_block = jnp.where(allowed, jnp.exp(scores - new_max[:, :, None]), 0.0)
        running_sum = running_sum * factor + jnp.sum(prob_block, axis=2)
        accumulated = accumulated * factor.T[:, :, None] + jnp.einsum(
            "hqk,khd->qhd",
            prob_block.astype(jnp.bfloat16),
            value_block,
            preferred_element_type=jnp.float32,
        )
        return (new_max, running_sum, accumulated)

    final_max, final_sum, accumulated = lax.fori_loop(
        0, piece_rows // block_rows, step, start_state
    )
    head_out = accumulated / final_sum.T[:, :, None]
    log_norm = (final_max + jnp.log(final_sum)).T
    mixed_heads = head_out.reshape(rows_here, model_width).astype(jnp.bfloat16)
    hidden = inputs + matmul(mixed_heads, full_proj)
    normed_two, inverse_two = norm_parts(hidden, gain_two)
    normed_two = normed_two.astype(jnp.bfloat16)
    router = jax.nn.softmax(matmul(normed_two, full_router), axis=-1)
    route_onehot = (
        routes[:, :, None] == jnp.arange(experts, dtype=jnp.int32)[None, None, :]
    ).astype(jnp.float32)
    picked = jnp.sum(route_onehot * router[:, None, :], axis=2)
    picked_total = jnp.sum(picked, axis=1, keepdims=True)
    gate_values = picked / picked_total
    flat_routes = routes.reshape(-1)
    flat_onehot = route_onehot.reshape(-1, experts).astype(jnp.int32)
    slot_ranks = jnp.sum((jnp.cumsum(flat_onehot, axis=0) - flat_onehot) * flat_onehot, axis=1)
    doubled = jnp.repeat(normed_two, 2, axis=0)
    outgoing = (
        jnp.zeros((experts, capacity, model_width), jnp.bfloat16)
        .at[flat_routes, slot_ranks]
        .set(doubled)
    )
    arrived = lax.all_to_all(
        outgoing.reshape(expert_count, local_experts * capacity, model_width),
        "expert",
        split_axis=0,
        concat_axis=0,
        tiled=True,
    )
    arrived = arrived.reshape(expert_count, local_experts, capacity, model_width)
    row_list = []
    pre_list = []
    act_list = []
    produced_list = []
    for slot_expert in range(local_experts):
        expert_rows = arrived[:, slot_expert].reshape(expert_count * capacity, model_width)
        pre_act = matmul(expert_rows, expert_first[slot_expert])
        activated = jax.nn.gelu(pre_act, approximate=False).astype(jnp.bfloat16)
        produced = matmul(activated, expert_second[slot_expert]).astype(jnp.bfloat16)
        row_list.append(expert_rows)
        pre_list.append(pre_act)
        act_list.append(activated)
        produced_list.append(produced.reshape(expert_count, 1, capacity, model_width))
    produced_all = jnp.concatenate(produced_list, axis=1).reshape(
        expert_count, local_experts * capacity, model_width
    )
    returned = lax.all_to_all(
        produced_all, "expert", split_axis=0, concat_axis=0, tiled=True
    ).reshape(experts, capacity, model_width)
    route_out = (
        returned[flat_routes, slot_ranks].reshape(rows_here, 2, model_width).astype(jnp.float32)
    )
    layer_out = hidden + jnp.sum(gate_values[:, :, None] * route_out, axis=1)
    grad_final = out_grad.astype(jnp.float32)
    grad_gates = jnp.sum(grad_final[:, None, :] * route_out, axis=2)
    grad_routes = (
        (gate_values[:, :, None] * grad_final[:, None, :])
        .astype(jnp.bfloat16)
        .reshape(-1, model_width)
    )
    grad_outgoing = (
        jnp.zeros((experts, capacity, model_width), jnp.bfloat16)
        .at[flat_routes, slot_ranks]
        .set(grad_routes)
    )
    grad_arrived = lax.all_to_all(
        grad_outgoing.reshape(expert_count, local_experts * capacity, model_width),
        "expert",
        split_axis=0,
        concat_axis=0,
        tiled=True,
    )
    grad_arrived = grad_arrived.reshape(expert_count, local_experts, capacity, model_width)
    grad_in_parts = []
    grad_out_parts = []
    back_list = []
    for slot_expert in range(local_experts):
        grad_rows = grad_arrived[:, slot_expert].reshape(expert_count * capacity, model_width)
        grad_act = contract_last(grad_rows, expert_second[slot_expert])
        grad_pre = (grad_act * gelu_slope(pre_list[slot_expert])).astype(jnp.bfloat16)
        grad_rows_in = contract_last(grad_pre, expert_first[slot_expert]).astype(jnp.bfloat16)
        back_list.append(grad_rows_in.reshape(expert_count, 1, capacity, model_width))
        grad_first = contract_first(row_list[slot_expert], grad_pre)
        grad_second = contract_first(act_list[slot_expert], grad_rows)
        grad_in_parts.append(grad_first)
        grad_out_parts.append(grad_second)
    grad_w_in, grad_w_out = (
        lax.psum_scatter(
            jnp.stack(grad_in_parts).astype(jnp.bfloat16), "shard", scatter_dimension=2, tiled=True
        ).astype(jnp.float32),
        lax.psum_scatter(
            jnp.stack(grad_out_parts).astype(jnp.bfloat16), "shard", scatter_dimension=1, tiled=True
        ).astype(jnp.float32),
    )
    back_all = jnp.concatenate(back_list, axis=1).reshape(
        expert_count, local_experts * capacity, model_width
    )
    sent_back = lax.all_to_all(back_all, "expert", split_axis=0, concat_axis=0, tiled=True).reshape(
        experts, capacity, model_width
    )
    grad_copies = (
        sent_back[flat_routes, slot_ranks].reshape(rows_here, 2, model_width).astype(jnp.float32)
    )
    weighted = jnp.sum(grad_gates * picked, axis=1, keepdims=True)
    grad_picked = grad_gates / picked_total - weighted / (picked_total * picked_total)
    grad_router = jnp.sum(grad_picked[:, :, None] * route_onehot, axis=1)
    grad_logits = (
        router * (grad_router - jnp.sum(router * grad_router, axis=1, keepdims=True))
    ).astype(jnp.bfloat16)
    grad_w_router = contract_first(normed_two, grad_logits)
    grad_normed_two = jnp.sum(grad_copies, axis=1) + contract_last(grad_logits, full_router)
    grad_norm_two, grad_gain_two = norm_back(hidden, inverse_two, gain_two, grad_normed_two)
    grad_hidden = grad_final + grad_norm_two
    grad_branch = grad_hidden.astype(jnp.bfloat16)
    grad_w_proj = contract_first(mixed_heads, grad_branch)
    grad_mixed = contract_last(grad_branch, full_proj).astype(jnp.bfloat16)
    row_dot = jnp.sum(
        grad_mixed.reshape(rows_here, head_count, head_width).astype(jnp.float32) * head_out, axis=2
    )
    all_log_norm, all_row_dot = (
        lax.all_gather(log_norm, "shard", axis=0, tiled=True),
        lax.all_gather(row_dot, "shard", axis=0, tiled=True),
    )
    key_heads = keys_here.reshape(rows_here, head_count, head_width)
    value_heads = values_here.reshape(rows_here, head_count, head_width)
    back_state = (
        jnp.zeros((rows_here, head_count, head_width), jnp.float32),
        jnp.zeros((rows_here, head_count, head_width), jnp.float32),
        jnp.zeros((seq_length, model_width), jnp.float32),
        jnp.zeros((bucket_count, head_count), jnp.float32),
    )
    piece_queries = lax.all_gather(queries, "shard", axis=0, tiled=True)
    piece_grads = lax.all_gather(grad_mixed, "shard", axis=0, tiled=True)
    piece_rows = piece_queries.shape[0]
    attend_block_rows = math.gcd(piece_rows, 512)

    def step(block_index, loop_state):
        grad_keys, grad_values, grad_queries, grad_bias = loop_state
        offset = block_index * attend_block_rows
        query_block = lax.dynamic_slice_in_dim(piece_queries, offset, attend_block_rows, 0).reshape(
            attend_block_rows, head_count, head_width
        )
        grad_block = lax.dynamic_slice_in_dim(piece_grads, offset, attend_block_rows, 0).reshape(
            attend_block_rows, head_count, head_width
        )
        query_pos = offset + jnp.arange(attend_block_rows, dtype=jnp.int32)
        query_seg = lax.dynamic_slice_in_dim(seq_segments, offset, attend_block_rows, 0)
        norm_block = lax.dynamic_slice_in_dim(all_log_norm, offset, attend_block_rows, 0)
        dot_block = lax.dynamic_slice_in_dim(all_row_dot, offset, attend_block_rows, 0)
        distance_bucket_table = bucket_block(query_pos, local_pos)
        bias_values = jnp.einsum(
            "yoc,yi->ioc",
            distance_bucket_table,
            position_bias_table,
            preferred_element_type=jnp.float32,
        )
        allowed = (
            (query_pos[:, None] >= local_pos[None, :]) & (query_seg[:, None] == local_seg[None, :])
        )[None]
        scores = (
            jnp.einsum("qhd,khd->hqk", query_block, key_heads, preferred_element_type=jnp.float32)
            * score_scale
            + bias_values
        )
        prob_block = jnp.where(allowed, jnp.exp(scores - norm_block.T[:, :, None]), 0.0)
        grad_values = grad_values + jnp.einsum(
            "hqk,qhd->khd",
            prob_block.astype(jnp.bfloat16),
            grad_block,
            preferred_element_type=jnp.float32,
        )
        grad_probs = jnp.einsum(
            "qhd,khd->hqk", grad_block, value_heads, preferred_element_type=jnp.float32
        )
        score_gradient = (prob_block * (grad_probs - dot_block.T[:, :, None])).astype(jnp.bfloat16)
        grad_keys = (
            grad_keys
            + jnp.einsum(
                "hqk,qhd->khd", score_gradient, query_block, preferred_element_type=jnp.float32
            )
            * score_scale
        )
        query_part = (
            jnp.einsum(
                "hqk,khd->qhd", score_gradient, key_heads, preferred_element_type=jnp.float32
            )
            * score_scale
        )
        grad_queries = lax.dynamic_update_slice_in_dim(
            grad_queries, query_part.reshape(attend_block_rows, model_width), offset, 0
        )
        grad_bias = grad_bias + jnp.einsum(
            "iof,mof->mi", score_gradient, distance_bucket_table, preferred_element_type=jnp.float32
        )
        return (grad_keys, grad_values, grad_queries, grad_bias)

    grad_keys, grad_values, grad_queries, grad_bias_table = lax.fori_loop(
        0, piece_rows // attend_block_rows, step, back_state
    )
    grad_query_here = lax.psum_scatter(
        grad_queries.astype(jnp.bfloat16), "shard", scatter_dimension=0, tiled=True
    )
    grad_key_here = grad_keys.reshape(rows_here, model_width).astype(jnp.bfloat16)
    grad_value_here = grad_values.reshape(rows_here, model_width).astype(jnp.bfloat16)
    grad_w_query = contract_first(normed_one, grad_query_here)
    grad_w_key = contract_first(normed_one, grad_key_here)
    grad_w_value = contract_first(normed_one, grad_value_here)
    grad_normed_one = (
        contract_last(grad_query_here, full_query)
        + contract_last(grad_key_here, full_key)
        + contract_last(grad_value_here, full_value)
    )
    grad_norm_one, grad_gain_one = norm_back(inputs, inverse_one, gain_one, grad_normed_one)
    tokens_grad = (grad_hidden + grad_norm_one).astype(jnp.bfloat16)
    shares = (
        lax.psum_scatter(
            grad_w_query.astype(jnp.bfloat16), "shard", scatter_dimension=0, tiled=True
        ).astype(jnp.float32),
        lax.psum_scatter(
            grad_w_key.astype(jnp.bfloat16), "shard", scatter_dimension=0, tiled=True
        ).astype(jnp.float32),
        lax.psum_scatter(
            grad_w_value.astype(jnp.bfloat16), "shard", scatter_dimension=0, tiled=True
        ).astype(jnp.float32),
        lax.psum_scatter(
            grad_w_proj.astype(jnp.bfloat16), "shard", scatter_dimension=0, tiled=True
        ).astype(jnp.float32),
        lax.psum_scatter(
            grad_w_router.astype(jnp.bfloat16), "shard", scatter_dimension=0, tiled=True
        ).astype(jnp.float32),
        lax.psum_scatter(
            grad_gain_one.astype(jnp.bfloat16), "shard", scatter_dimension=0, tiled=True
        ).astype(jnp.float32),
        lax.psum_scatter(
            grad_gain_two.astype(jnp.bfloat16), "shard", scatter_dimension=0, tiled=True
        ).astype(jnp.float32),
        lax.psum_scatter(
            grad_bias_table.astype(jnp.bfloat16), "shard", scatter_dimension=0, tiled=True
        ).astype(jnp.float32),
    )
    totals = (
        lax.psum(shares[0].astype(jnp.bfloat16), "expert").astype(jnp.float32),
        lax.psum(shares[1].astype(jnp.bfloat16), "expert").astype(jnp.float32),
        lax.psum(shares[2].astype(jnp.bfloat16), "expert").astype(jnp.float32),
        lax.psum(shares[3].astype(jnp.bfloat16), "expert").astype(jnp.float32),
        lax.psum(shares[4].astype(jnp.bfloat16), "expert").astype(jnp.float32),
        lax.psum(shares[5].astype(jnp.bfloat16), "expert").astype(jnp.float32),
        lax.psum(shares[6].astype(jnp.bfloat16), "expert").astype(jnp.float32),
        lax.psum(shares[7].astype(jnp.bfloat16), "expert").astype(jnp.float32),
    )
    return (
        layer_out.astype(jnp.bfloat16),
        tokens_grad,
        totals[0],
        totals[1],
        totals[2],
        totals[3],
        totals[4],
        totals[5],
        totals[6],
        totals[7],
        grad_w_in,
        grad_w_out,
    )


VMEM_BYTES = 60 * 1024 * 1024
TILE = 256
PACK_ROWS = 16
DENSE_TOKENS = 16384


def attend_forward(qkv_ref, skew_ref, seg_col_ref, seg_row_ref, out_ref, prob_ref, toeplitz):
    heads, seq_length = prob_ref.shape[0], prob_ref.shape[1]
    width = out_ref.shape[1] // heads
    tiles = seq_length // TILE
    scale = width ** (-0.5)
    lower = lax.broadcasted_iota(jnp.int32, (TILE, TILE), 0) >= lax.broadcasted_iota(
        jnp.int32, (TILE, TILE), 1
    )
    for head in range(heads):
        for delta in range(tiles):
            row = skew_ref[head, delta : delta + 1, :]
            wide = jnp.broadcast_to(row, (TILE, 2 * TILE))
            turned = pltpu.roll(wide, 0, 1, stride=1, stride_axis=0)[:, :TILE]
            if delta == 0:
                turned = jnp.where(lower, turned, NEG_BIG)
            toeplitz[delta] = turned
        query_cols = pl.ds(head * width, width)
        key_cols = pl.ds((heads + head) * width, width)
        value_cols = pl.ds((2 * heads + head) * width, width)
        for tile in range(tiles):
            rows = pl.ds(tile * TILE, TILE)
            extent = (tile + 1) * TILE
            query = qkv_ref[rows, query_cols]
            scores = contract_last(query, qkv_ref[pl.ds(0, extent), key_cols]) * scale
            bias = jnp.concatenate([toeplitz[tile - other] for other in range(tile + 1)], axis=1)
            same = seg_col_ref[rows, :] == seg_row_ref[:, pl.ds(0, extent)]
            scores = jnp.where(same, scores + bias, NEG_BIG)
            top = jnp.max(scores, axis=1, keepdims=True)
            weight = jnp.exp(scores - top)
            total = jnp.sum(weight, axis=1, keepdims=True)
            prob = (weight * (1.0 / total)).astype(jnp.bfloat16)
            prob_ref[head, rows, pl.ds(0, extent)] = prob
            out_ref[rows, query_cols] = matmul(
                prob, qkv_ref[pl.ds(0, extent), value_cols]
            ).astype(jnp.bfloat16)


def attend_backward(qkv_ref, grad_ref, prob_ref, grad_qkv_ref, diag_ref, keys_acc, values_acc, blocks):
    heads, seq_length = prob_ref.shape[0], prob_ref.shape[1]
    width = grad_ref.shape[1] // heads
    tiles = seq_length // TILE
    scale = width ** (-0.5)
    flip = (
        lax.broadcasted_iota(jnp.int32, (TILE, TILE), 0)
        + lax.broadcasted_iota(jnp.int32, (TILE, TILE), 1)
        == TILE - 1
    ).astype(jnp.float32)
    for head in range(heads):
        query_cols = pl.ds(head * width, width)
        key_cols = pl.ds((heads + head) * width, width)
        value_cols = pl.ds((2 * heads + head) * width, width)
        keys_acc[...] = jnp.zeros_like(keys_acc)
        values_acc[...] = jnp.zeros_like(values_acc)
        blocks[...] = jnp.zeros_like(blocks)
        for tile in range(tiles):
            rows = pl.ds(tile * TILE, TILE)
            extent = (tile + 1) * TILE
            seen = pl.ds(0, extent)
            query = qkv_ref[rows, query_cols]
            grad = grad_ref[rows, query_cols]
            prob = prob_ref[head, rows, seen]
            wide = prob.astype(jnp.float32)
            grad_prob = contract_last(grad, qkv_ref[seen, value_cols])
            dots = jnp.sum(wide * grad_prob, axis=1, keepdims=True)
            grad_score = (wide * (grad_prob - dots)).astype(jnp.bfloat16)
            grad_qkv_ref[rows, query_cols] = (
                matmul(grad_score, qkv_ref[seen, key_cols]) * scale
            ).astype(jnp.bfloat16)
            keys_acc[seen, :] += contract_first(grad_score, query)
            values_acc[seen, :] += contract_first(prob, grad)
            for other in range(tile + 1):
                blocks[tile - other] += grad_score[:, other * TILE : (other + 1) * TILE].astype(
                    jnp.float32
                )
        grad_qkv_ref[:, key_cols] = (keys_acc[...] * scale).astype(jnp.bfloat16)
        grad_qkv_ref[:, value_cols] = values_acc[...].astype(jnp.bfloat16)
        for delta in range(tiles):
            flipped = jnp.dot(
                flip,
                blocks[delta],
                precision=lax.Precision.HIGHEST,
                preferred_element_type=jnp.float32,
            )
            padded = jnp.concatenate([flipped, jnp.zeros_like(flipped)], axis=1)
            turned = pltpu.roll(padded, 0, 1, stride=1, stride_axis=0)
            diag_ref[head, delta : delta + 1, :] = jnp.sum(turned, axis=0, keepdims=True)


def expert_step(
    ranks_ref,
    gates_ref,
    rows_ref,
    grads_ref,
    first_ref,
    second_ref,
    out_ref,
    back_ref,
    dots_ref,
    grad_first_ref,
    grad_second_ref,
):
    local_experts, group, _, block = ranks_ref.shape
    capacity = 64 * block // 256

    @pl.when(pl.program_id(0) == 0)
    def _():
        grad_first_ref[...] = jnp.zeros_like(grad_first_ref)
        grad_second_ref[...] = jnp.zeros_like(grad_second_ref)

    slot = lax.broadcasted_iota(jnp.int32, (capacity, block), 0).astype(jnp.float32)
    for expert in range(local_experts):
        picks = [ranks_ref[expert, at] == slot for at in range(group)]
        ones = [pick.astype(jnp.float32).astype(jnp.bfloat16) for pick in picks]
        gate = jnp.concatenate(
            [
                jnp.sum(jnp.where(picks[at], gates_ref[expert, at], 0.0), axis=1, keepdims=True)
                for at in range(group)
            ],
            axis=0,
        )
        rows = jnp.concatenate(
            [matmul(ones[at], rows_ref[at]).astype(jnp.bfloat16) for at in range(group)], axis=0
        )
        grads = jnp.concatenate(
            [matmul(ones[at], grads_ref[at, pl.ds(0, block), :]) for at in range(group)], axis=0
        )
        pre = matmul(rows, first_ref[expert])
        half = 0.5 * (1.0 + lax.erf(pre * 0.7071067811865476))
        act = (pre * half).astype(jnp.bfloat16)
        slope = half + pre * jnp.exp(-0.5 * pre * pre) * 0.3989422804014327
        produced = matmul(act, second_ref[expert])
        dots = jnp.sum(grads * produced, axis=1, keepdims=True)
        given = (gate * grads).astype(jnp.bfloat16)
        weighted = (gate * produced).astype(jnp.bfloat16)
        grad_pre = (contract_last(given, second_ref[expert]) * slope).astype(jnp.bfloat16)
        back = contract_last(grad_pre, first_ref[expert]).astype(jnp.bfloat16)
        grad_first_ref[expert] += contract_first(rows, grad_pre)
        grad_second_ref[expert] += contract_first(act, given)
        for at in range(group):
            part = slice(at * capacity, (at + 1) * capacity)
            out_part = contract_first(ones[at], weighted[part])
            back_part = contract_first(ones[at], back[part])
            if expert > 0:
                out_part = out_part + out_ref[at].astype(jnp.float32)
                back_part = back_part + back_ref[at].astype(jnp.float32)
            out_ref[at] = out_part.astype(jnp.bfloat16)
            back_ref[at] = back_part.astype(jnp.bfloat16)
            dots_ref[expert, at] = jnp.sum(
                jnp.where(picks[at], dots[part], 0.0), axis=0, keepdims=True
            )


def run_experts(ranks, gates, rows, grads, first, second):
    local_experts, blocks, _, block = ranks.shape
    width = rows.shape[2]
    group = math.gcd(blocks, 4)
    small = pl.BlockSpec((local_experts, group, 1, block), lambda i: (0, i, 0, 0))
    fixed = lambda shape: pl.BlockSpec(
        shape, lambda i: (0, 0, 0), pipeline_mode=pl.Buffered(1)
    )
    tall = pl.BlockSpec((group, block, width), lambda i: (i, 0, 0))
    return pl.pallas_call(
        expert_step,
        grid=(blocks // group,),
        in_specs=[
            small,
            small,
            tall,
            pl.BlockSpec((group, grads.shape[1], width), lambda i: (i, 0, 0)),
            fixed(first.shape),
            fixed(second.shape),
        ],
        out_specs=[tall, tall, small, fixed(first.shape), fixed(second.shape)],
        out_shape=[
            jax.ShapeDtypeStruct((blocks, block, width), jnp.bfloat16),
            jax.ShapeDtypeStruct((blocks, block, width), jnp.bfloat16),
            jax.ShapeDtypeStruct(ranks.shape, jnp.float32),
            jax.ShapeDtypeStruct(first.shape, jnp.float32),
            jax.ShapeDtypeStruct(second.shape, jnp.float32),
        ],
        compiler_params=pltpu.CompilerParams(vmem_limit_bytes=VMEM_BYTES),
    )(ranks, gates, rows, grads, first, second)


def pad_rows(flat, rows, width):
    return jnp.concatenate(
        [flat, jnp.zeros((rows * width - flat.shape[0],), flat.dtype)]
    ).reshape(rows, width)


def dense_plan(
    tokens,
    w_query,
    w_key,
    w_value,
    w_out_attn,
    w_router,
    gain_attn,
    gain_moe,
    rel_bias,
    w_in,
    w_out,
    out_grad,
    routes,
    segments,
    buckets,
):
    block, width = tokens.shape
    shards = lax.axis_size("shard")
    groups = lax.axis_size("expert")
    seq_length = block * shards
    head_count = rel_bias.shape[1]
    heads = head_count // shards
    head_width = width // head_count
    owned = heads * head_width
    experts = w_router.shape[1]
    local_experts = w_in.shape[0]
    bucket_count = rel_bias.shape[0] * shards
    part_rows = w_router.shape[0]
    blocks = groups * shards
    tiles = seq_length // TILE
    shard_at = lax.axis_index("shard")
    expert_at = lax.axis_index("expert")
    bf16, f32 = jnp.bfloat16, jnp.float32

    small = jnp.concatenate(
        [w_router.reshape(-1), gain_attn.reshape(-1), gain_moe.reshape(-1), rel_bias.reshape(-1)]
    )
    opening = jnp.concatenate([tokens, pad_rows(small, PACK_ROWS, width)], axis=0)
    opened = lax.all_gather(opening, "shard", axis=0)
    tokens_seq = opened[:, :block].reshape(seq_length, width)
    smalls = opened[:, block:].reshape(shards, -1)
    at = part_rows * experts
    full_router = smalls[:, :at].reshape(width, experts)
    gain_one = smalls[:, at : at + part_rows].reshape(width).astype(f32)
    gain_two = smalls[:, at + part_rows : at + 2 * part_rows].reshape(width).astype(f32)
    at = at + 2 * part_rows
    table = smalls[:, at : at + rel_bias.size].reshape(bucket_count, head_count)

    stacked = jnp.stack([w_query, w_key, w_value], axis=1).reshape(part_rows, 3, shards, owned)
    stacked = stacked.transpose(2, 0, 1, 3).reshape(shards, part_rows, 3 * owned)
    copies = jnp.broadcast_to(w_out_attn[None], (shards,) + w_out_attn.shape)
    weights = lax.all_to_all(
        jnp.concatenate([stacked, copies], axis=2), "shard", split_axis=0, concat_axis=0, tiled=True
    )
    own_qkv = weights[:, :, : 3 * owned].reshape(width, 3 * owned)
    full_proj = weights[:, :, 3 * owned :].reshape(width, width)

    closing = jnp.concatenate(
        [out_grad, pad_rows(routes.T.reshape(-1).astype(bf16), PACK_ROWS, width)], axis=0
    )
    closed = lax.all_gather(closing, ("expert", "shard"), axis=0)

    inputs_seq = tokens_seq.astype(f32)
    normed_seq, inverse_seq = norm_parts(inputs_seq, gain_one)
    normed_seq = normed_seq.astype(bf16)
    qkv = matmul(normed_seq, own_qkv).astype(bf16)
    bucket_hot = (buckets[:, None] == jnp.arange(bucket_count, dtype=jnp.int32)[None, :]).astype(bf16)
    own_table = lax.dynamic_slice_in_dim(table, shard_at * heads, heads, 1)
    by_distance = lax.dot_general(
        own_table, bucket_hot, (((0,), (1,)), ((), ())), preferred_element_type=f32
    )
    descending = jnp.pad(by_distance, ((0, 0), (TILE, TILE)))[:, ::-1]
    pieces = []
    for delta in range(tiles):
        low_at = seq_length + TILE - 1 - delta * TILE
        pieces.append(
            jnp.concatenate(
                [descending[:, low_at : low_at + TILE], descending[:, low_at - TILE : low_at]], axis=1
            )
        )
    skew = jnp.stack(pieces, axis=1)
    seg = segments[0]
    mixed, prob = pl.pallas_call(
        attend_forward,
        out_shape=[
            jax.ShapeDtypeStruct((seq_length, owned), bf16),
            jax.ShapeDtypeStruct((heads, seq_length, seq_length), bf16),
        ],
        scratch_shapes=[pltpu.VMEM((tiles, TILE, TILE), f32)],
        compiler_params=pltpu.CompilerParams(vmem_limit_bytes=VMEM_BYTES),
    )(qkv, skew, seg[:, None], seg[None, :])
    mixed_here = lax.all_to_all(
        mixed.reshape(shards, block, owned), "shard", split_axis=0, concat_axis=0, tiled=True
    )
    mixed_here = mixed_here.transpose(1, 0, 2).reshape(block, width)

    inputs = tokens.astype(f32)
    hidden = inputs + matmul(mixed_here, full_proj)
    normed_two, inverse_two = norm_parts(hidden, gain_two)
    normed_two = normed_two.astype(bf16)
    normed_all = lax.all_gather(normed_two, ("expert", "shard"), axis=0)
    expert_ids = jnp.arange(experts, dtype=jnp.int32)

    grads_all = closed
    routes_all = closed[:, block].reshape(blocks, width)[:, : 2 * block]
    routes_all = routes_all.reshape(blocks, 2, block).astype(jnp.int32)
    logits_all = lax.dot_general(
        full_router, normed_all, (((0,), (2,)), ((), ())), preferred_element_type=f32
    )
    router_all = jax.nn.softmax(logits_all, axis=0)
    own_ids = expert_at * local_experts + jnp.arange(local_experts, dtype=jnp.int32)
    named = (routes_all[None] == own_ids[:, None, None, None]).any(axis=2)
    first_hot = routes_all[None, :, 0] == expert_ids[:, None, None]
    second_hot = routes_all[None, :, 1] == expert_ids[:, None, None]
    picked_sum = jnp.sum(jnp.where(first_hot | second_hot, router_all, 0.0), axis=0)
    own_router = lax.dynamic_slice_in_dim(router_all, expert_at * local_experts, local_experts, 0)
    gates_all = jnp.where(named, own_router / picked_sum[None], 0.0)
    before = (jnp.arange(block)[:, None] < jnp.arange(block)[None, :]).astype(bf16)
    ranks = matmul(named.astype(bf16).reshape(-1, block), before).reshape(named.shape)
    ranks = jnp.where(named, ranks, -1.0)
    out_parts, back_parts, dots, grad_w_in, grad_w_out = run_experts(
        ranks[:, :, None, :], gates_all[:, :, None, :], normed_all, grads_all, w_in, w_out
    )
    dots = dots[:, :, 0, :]
    dots_by_choice = jnp.sum(
        jnp.where(routes_all[None] == own_ids[:, None, None, None], dots[:, :, None, :], 0.0), axis=0
    )
    dots_rows = jnp.pad(
        dots_by_choice.astype(bf16).reshape(blocks, 1, 2 * block),
        ((0, 0), (0, PACK_ROWS - 1), (0, width - 2 * block)),
    )
    back_parts = jnp.concatenate([back_parts, dots_rows], axis=1)
    back_here = lax.psum_scatter(back_parts, ("expert", "shard"), scatter_dimension=0, tiled=True)[0]

    router = jax.nn.softmax(matmul(normed_two, full_router), axis=-1)
    route_onehot = (routes[:, :, None] == expert_ids[None, None, :]).astype(f32)
    picked = jnp.sum(route_onehot * router[:, None, :], axis=2)
    picked_total = jnp.sum(picked, axis=1, keepdims=True)
    grad_gates = back_here[block, : 2 * block].reshape(2, block).T.astype(f32)
    weighted = jnp.sum(grad_gates * picked, axis=1, keepdims=True)
    grad_picked = grad_gates / picked_total - weighted / (picked_total * picked_total)
    grad_router = jnp.sum(grad_picked[:, :, None] * route_onehot, axis=1)
    grad_logits = (
        router * (grad_router - jnp.sum(router * grad_router, axis=1, keepdims=True))
    ).astype(bf16)
    grad_w_router = contract_first(normed_two, grad_logits)
    grad_normed_two = back_here[:block].astype(f32) + contract_last(grad_logits, full_router)
    grad_norm_two, grad_gain_two = norm_back(hidden, inverse_two, gain_two, grad_normed_two)
    grad_hidden = out_grad.astype(f32) + grad_norm_two
    grad_branch = lax.all_gather(grad_hidden.astype(bf16), "shard", axis=0, tiled=True)

    out_parts, grad_branch = lax.optimization_barrier((out_parts, grad_branch))
    out_here = lax.psum_scatter(out_parts, ("expert", "shard"), scatter_dimension=0, tiled=True)[0]
    layer_out = (hidden + out_here.astype(f32)).astype(bf16)

    grad_w_proj = contract_first(mixed, grad_branch)
    grad_mixed = contract_last(grad_branch, w_out_attn).astype(bf16)
    grad_qkv, diagonals = pl.pallas_call(
        attend_backward,
        out_shape=[
            jax.ShapeDtypeStruct((seq_length, 3 * owned), bf16),
            jax.ShapeDtypeStruct((heads, tiles, 2 * TILE), f32),
        ],
        scratch_shapes=[
            pltpu.VMEM((seq_length, head_width), f32),
            pltpu.VMEM((seq_length, head_width), f32),
            pltpu.VMEM((tiles, TILE, TILE), f32),
        ],
        compiler_params=pltpu.CompilerParams(vmem_limit_bytes=VMEM_BYTES),
    )(qkv, grad_mixed, prob)
    grad_normed_one = contract_last(grad_qkv, own_qkv)
    norm_one_here = lax.psum_scatter(
        grad_normed_one.astype(bf16), "shard", scatter_dimension=0, tiled=True
    ).astype(f32)
    grad_gain_one = jnp.sum(grad_normed_one * inputs_seq * inverse_seq, axis=0)
    by_distance_grad = jnp.zeros((heads, seq_length + TILE), f32)
    for delta in range(tiles):
        piece = diagonals[:, delta, ::-1]
        start = delta * TILE
        by_distance_grad = by_distance_grad.at[:, start : start + 2 * TILE].add(piece)
    by_distance_grad = by_distance_grad[:, TILE : TILE + seq_length]
    grad_table = lax.dot_general(
        bucket_hot.astype(f32),
        by_distance_grad,
        (((0,), (1,)), ((), ())),
        precision=lax.Precision.HIGHEST,
        preferred_element_type=f32,
    )
    grad_qkv_full = contract_first(normed_seq, grad_qkv)

    bias_rows = grad_table.reshape(shards, -1)
    tail = jnp.concatenate(
        [
            grad_w_router.reshape(shards, -1),
            grad_gain_one.reshape(shards, -1),
            grad_gain_two.reshape(shards, -1),
            bias_rows,
        ],
        axis=1,
    )
    tail_rows = -(-tail.shape[1] // (3 * owned))
    tail_rows = -(-tail_rows // 16) * 16
    tail = jnp.pad(tail, ((0, 0), (0, tail_rows * 3 * owned - tail.shape[1])))
    leaving = jnp.concatenate(
        [
            grad_qkv_full.reshape(shards, part_rows, 3 * owned),
            tail.reshape(shards, tail_rows, 3 * owned),
        ],
        axis=1,
    ).astype(bf16)
    landed = lax.all_to_all(leaving, "shard", split_axis=0, concat_axis=0, tiled=True)
    landed_tail = landed[:, part_rows:].reshape(shards, -1)
    plain = part_rows * (experts + 2)
    summed_tail = jnp.sum(landed_tail[:, :plain].astype(f32), axis=0).astype(bf16)
    bias_count = rel_bias.shape[0] * heads
    final = jnp.concatenate(
        [
            landed[:, :part_rows].reshape(-1),
            grad_w_proj.astype(bf16).reshape(-1),
            summed_tail,
            landed_tail[:, plain : plain + bias_count].reshape(-1),
        ]
    )
    length = final.shape[0]
    final = jnp.pad(final, (0, -length % 2048)).reshape(-1, 128)
    final = lax.psum(final, "expert").reshape(-1).astype(f32)
    size = part_rows * width
    grads_qkv = final[: 3 * size].reshape(shards, part_rows, 3, owned)
    grads_qkv = grads_qkv.transpose(2, 1, 0, 3).reshape(3, part_rows, width)
    proj_total = final[3 * size : 4 * size].reshape(part_rows, width)
    rest = final[4 * size : length]
    router_total = rest[: part_rows * experts].reshape(part_rows, experts)
    gain_one_total = rest[part_rows * experts : part_rows * (experts + 1)]
    gain_two_total = rest[part_rows * (experts + 1) : plain]
    bias_total = rest[plain:].reshape(shards, rel_bias.shape[0], heads)
    bias_total = bias_total.transpose(1, 0, 2).reshape(rel_bias.shape)

    inverse_one = lax.rsqrt(jnp.mean(inputs * inputs, axis=-1, keepdims=True) + EPSILON)
    grad_norm_one, _ = norm_back(inputs, inverse_one, gain_one, norm_one_here)
    tokens_grad = (grad_hidden + grad_norm_one).astype(bf16)
    return (
        layer_out,
        tokens_grad,
        grads_qkv[0],
        grads_qkv[1],
        grads_qkv[2],
        proj_total,
        router_total,
        gain_one_total,
        gain_two_total,
        bias_total,
        grad_w_in,
        grad_w_out,
    )


def per_device(*arguments):
    tokens, rel_bias = arguments[0], arguments[8]
    shards = lax.axis_size("shard")
    every = tokens.shape[0] * shards * lax.axis_size("expert")
    if every > DENSE_TOKENS or rel_bias.shape[1] % shards or tokens.shape[0] % TILE:
        return routed_plan(*arguments)
    return dense_plan(*arguments)


def solution(mesh):
    placed = (
        P(("expert", "shard"), None),
        P("shard", None),
        P("shard", None),
        P("shard", None),
        P("shard", None),
        P("shard", None),
        P("shard"),
        P("shard"),
        P("shard", None),
        P("expert", None, "shard"),
        P("expert", "shard", None),
        P(("expert", "shard"), None),
        P(("expert", "shard"), None),
        P("expert", None),
        P(),
    )
    return jax.shard_map(
        per_device,
        mesh=mesh,
        in_specs=placed,
        out_specs=(
            P(("expert", "shard"), None),
            P(("expert", "shard"), None),
            P("shard", None),
            P("shard", None),
            P("shard", None),
            P("shard", None),
            P("shard", None),
            P("shard"),
            P("shard"),
            P("shard", None),
            P("expert", None, "shard"),
            P("expert", "shard", None),
        ),
        check_vma=False,
    )
```
